32 devices in a mesh: band: 4 (over y, x), tile: 4 (over z), slab: 2 (over core).
Axes of the slice: x: 2, y: 2, z: 4, core: 2. Of those that a mesh axis runs over, the one named last changes fastest.
Arguments:
- strength: float32 [32], P('band'), may hold values from 0.0005 to 0.5
- opacity: float32 [16, 64, 256], P('slab', 'tile'), may hold values from 0.5 to 2
- planck: float32 [16, 64, 256], P('slab', 'tile'), may hold values from 0.5 to 2
- old_populations: float32 [5, 16, 64, 256], P(None, 'slab', 'tile'), may hold values from 0.1 to 1
- line_index: int32 [32], P('band'), may hold values from 0 to 4
- line_weight: float32 [32], P('band'), may hold values from 0.2 to 1
Outputs:
- new_populations: float32 [5, 16, 64, 256], P(None, 'slab', 'tile', 'band')
- new_source: float32 [32, 16, 64, 256], P('band', 'slab', 'tile')
The draws below stay inside these ranges and needn't reach their ends.
Inputs may be any that keep to these rules, and one draw needn't show every extreme that they name: line_index names a transition of the model atom.
All inputs are finite; a program needn't handle non-finite values.
Results may differ from the reference program's by a relative error of at most 0.0001.
Values sent between devices are 32-bit elements; how exact they have to be, the bound alone decides.
A program may use at most 64 MiB of HBM per device.

```python
import math
import jax
import jax.numpy as jnp
from jax import lax

YCELLS = 256
LINES = 5
LEVELS = 5
NX = 64
NZ = 16
FREQS = 32


def with_ends(result, key, least, largest):
    extent = result.shape
    index_at = [jax.random.randint(jax.random.fold_in(key, axis), (), 0, extent[axis]) for axis in range(len(extent))]
    result = result.at[tuple(index_at)].set(least)
    longest = extent.index(max(extent))
    index_at[longest] = (index_at[longest] + 1) % extent[longest]
    return result.at[tuple(index_at)].set(largest)


def level_of(rng, shape, pieces, smallest, high):
    loudness = 1.0
    for axis_at, shards_of in pieces:
        steps = jax.random.uniform(jax.random.fold_in(jax.random.fold_in(rng, 6), axis_at), (shards_of,), jnp.float32, smallest / len(pieces), high / len(pieces))
        loudness = loudness * jnp.repeat(jnp.exp(steps), shape[axis_at] // shards_of).reshape((-1,) + (1,) * (len(shape) - 1 - axis_at))
    return loudness


def setup_inputs(seed: int = 0) -> dict:
    key_list = jax.random.split(jax.random.key(seed), 7)
    return {
        "strength": jnp.clip(jnp.exp(math.log(0.5) - 6.9077552 * jax.random.uniform(key_list[0], (FREQS,), jnp.float32) ** level_of(key_list[0], (FREQS,), ((0, 4),), -0.2, 0.2)), 0.0005, 0.5),
        "opacity": jnp.clip(jnp.exp(math.log(2.0) - 1.3862944 * jax.random.uniform(key_list[1], (NZ, NX, YCELLS), jnp.float32) ** level_of(key_list[1], (NZ, NX, YCELLS), ((0, 2), (1, 4)), -0.2, 0.2)), 0.5, 2.0),
        "planck": jnp.clip(0.5 + 1.5 * jax.random.uniform(key_list[2], (NZ, NX, YCELLS), jnp.float32) ** level_of(key_list[2], (NZ, NX, YCELLS), ((0, 2), (1, 4)), -0.2, 0.2), 0.5, 2.0),
        "old_populations": jnp.clip(0.1 + 0.9 * jax.random.uniform(key_list[3], (LEVELS, NZ, NX, YCELLS), jnp.float32) ** level_of(key_list[3], (LEVELS, NZ, NX, YCELLS), ((1, 2), (2, 4)), -0.2, 0.2), 0.1, 1.0),
        "line_index": with_ends(jax.random.randint(key_list[4], (FREQS,), 0, LINES), jax.random.fold_in(key_list[4], 1), 0, LINES - 1).astype(jnp.int32),
        "line_weight": jnp.clip(0.2 + 0.8 * jax.random.uniform(key_list[5], (FREQS,), jnp.float32) ** level_of(key_list[5], (FREQS,), ((0, 4),), -0.2, 0.2), 0.2, 1.0),
    }


EPS_THERMAL = 0.1
COLLISION = 0.5
PATH_FACTOR = 1.25
TILT_SHARE = 0.4
LOWER_LEVEL = (0, 0, 1, 1, 2)
UPPER_LEVEL = (3, 4, 3, 4, 4)


def line_sources(levels_now):
    return jnp.stack([levels_now[UPPER_LEVEL[t]] / (levels_now[LOWER_LEVEL[t]] + levels_now[UPPER_LEVEL[t]]) for t in range(5)], axis=0)


def relax(jbar, planck):
    ratios = (jbar + COLLISION * planck[None]) / (1.0 + jbar + COLLISION)
    ground = jnp.ones_like(planck)
    level_three = ratios[0]
    level_four = ratios[1]
    level_one = 0.5 * (level_three / ratios[2] + level_four / ratios[3])
    level_two = level_four / ratios[4]
    stacked = jnp.stack([ground, level_one, level_two, level_three, level_four], axis=0)
    return stacked / jnp.sum(stacked, axis=0)


def reference(strength, opacity, planck, old_populations, line_index, line_weight):
    highest = lax.Precision.HIGHEST
    onehot = (line_index[:, None] == jnp.arange(LINES, dtype=jnp.int32)[None, :]).astype(jnp.float32)
    weighted = onehot * line_weight[:, None] * (LINES / (2.0 * FREQS))
    line_now = jnp.moveaxis(line_sources(old_populations), 1, 0)

    def layer_step(intensity, inputs):
        opacity_now, planck_now, lines_here = inputs
        source_now = EPS_THERMAL * planck_now[None] + (1.0 - EPS_THERMAL) * jnp.einsum("ft,txy->fxy", onehot, lines_here, precision=highest)
        attenuation = jnp.exp(-PATH_FACTOR * strength[:, None, None] * opacity_now[None])[:, None]
        zero_column = jnp.zeros_like(intensity[:, 0, :1])
        from_left = jnp.concatenate([zero_column, intensity[:, 0, :-1]], axis=1)
        from_right = jnp.concatenate([intensity[:, 1, 1:], zero_column], axis=1)
        upwind = jnp.stack([from_left, from_right], axis=1)
        intensity = attenuation * ((1.0 - TILT_SHARE) * intensity + TILT_SHARE * upwind) + (1.0 - attenuation) * source_now[:, None]
        rates_now = jnp.einsum("ft,fxy->txy", weighted, jnp.sum(intensity, axis=1), precision=highest)
        return intensity, rates_now

    start = jnp.zeros((FREQS, 2, NX, YCELLS), jnp.float32)
    _, rates = lax.scan(layer_step, start, (opacity, planck, line_now))
    jbar = jnp.moveaxis(rates, 0, 1)
    new_populations = relax(jbar, planck)
    new_source = EPS_THERMAL * planck[None] + (1.0 - EPS_THERMAL) * jnp.einsum("ft,tzxy->fzxy", onehot, line_sources(new_populations), precision=highest)
    return new_populations, new_source
```

```python
import functools

import jax
import jax.numpy as jnp
from jax import lax
from jax.experimental import pallas as pl
from jax.experimental.pallas import tpu as pltpu
from jax.sharding import PartitionSpec as P

MESH = pl.DeviceIdType.MESH
LINES = 5
LEVELS = 5
EPS_THERMAL = 0.1
COLLISION = 0.5
PATH_FACTOR = 1.25
TILT_SHARE = 0.4
LOWER_LEVEL = (0, 0, 1, 1, 2)
UPPER_LEVEL = (3, 4, 3, 4, 4)
LANES = 128
ROWS = 8
HALF = LANES // 2
BATCH = 4


def half_turn(v):
    return pltpu.roll(v, HALF, 1)


def kernel(
    sizes,
    strength,
    line_index,
    line_weight,
    opacity,
    planck,
    populations,
    pops_out,
    source_out,
    fields,
    planck_all,
    par_f,
    par_i,
    par_s,
    halo_out,
    halo_in,
    opac,
    src,
    plk,
    face_in,
    face_halo,
    face_out,
    acc,
    gathered,
    new_src,
    in_sem,
    idx_sem,
    par_send,
    par_recv,
    halo_send,
    halo_recv,
    face_send,
    face_recv,
    gat_send,
    gat_recv,
):
    bands, tiles, slabs, depth, freqs = sizes
    pairs = depth // 2
    subs = freqs // BATCH
    band = lax.axis_index("band")
    tile = lax.axis_index("tile")
    slab = lax.axis_index("slab")
    has_left = tile > 0
    has_right = tile < tiles - 1
    has_up = slab > 0
    has_down = slab < slabs - 1

    column = pl.multiple_of((band // 2) * LANES, LANES)
    loads = [
        pltpu.make_async_copy(opacity.at[:, :, pl.ds(column, LANES)], fields.at[0], in_sem.at[0]),
        pltpu.make_async_copy(planck.at[:, :, pl.ds(column, LANES)], fields.at[1], in_sem.at[1]),
        pltpu.make_async_copy(
            populations.at[:, :, :, pl.ds(column, LANES)], fields.at[pl.ds(2, LEVELS)], in_sem.at[2]
        ),
        pltpu.make_async_copy(planck, planck_all, in_sem.at[3]),
    ]
    for load in loads:
        load.start()

    barrier = pltpu.get_barrier_semaphore()
    for k in range(1, bands):
        pl.semaphore_signal(
            barrier, inc=1, device_id={"band": lax.rem(band + k, bands)}, device_id_type=MESH
        )
    expected = jnp.int32(bands - 1)
    for dt in (-1, 0, 1):
        for ds in (-1, 0, 1):
            if dt == 0 and ds == 0:
                continue
            there = (tile + dt >= 0) & (tile + dt < tiles) & (slab + ds >= 0) & (slab + ds < slabs)

            @pl.when(there)
            def _():
                pl.semaphore_signal(
                    barrier,
                    inc=1,
                    device_id={"tile": tile + dt, "slab": slab + ds},
                    device_id_type=MESH,
                )

            expected = expected + there.astype(jnp.int32)

    row = lax.broadcasted_iota(jnp.int32, (ROWS, LANES), 0)
    lane = lax.broadcasted_iota(jnp.int32, (ROWS, LANES), 1)
    left = lane < HALF
    own = (lane // HALF) == lax.rem(band, 2)
    top_left = left & (row == 0)
    low_right = jnp.logical_not(left) & (row == ROWS - 1)

    lane_row = lax.broadcasted_iota(jnp.int32, (1, LANES), 1)
    indices = jnp.zeros((1, LANES), jnp.int32)
    zero = jnp.zeros((ROWS, LANES), jnp.float32)
    rate, weight, which = zero, zero, zero
    for f in range(freqs):
        here = row == f
        rate = jnp.where(here, -PATH_FACTOR * strength[f], rate)
        weight = jnp.where(here, line_weight[f] * (LINES / (2.0 * freqs * bands)), weight)
        which = jnp.where(here, line_index[f].astype(jnp.float32), which)
        indices = jnp.where(lane_row == f, line_index[f], indices)
    par_f[0, 0] = rate
    par_f[0, 1] = weight
    par_f[0, 2] = which
    par_i[0] = indices

    @pl.when(jnp.logical_not(has_left))
    def _():
        halo_in[0] = jnp.zeros(halo_in.shape[1:], jnp.float32)
        face_halo[0] = jnp.zeros(face_halo.shape[1:], jnp.float32)

    @pl.when(jnp.logical_not(has_right))
    def _():
        halo_in[1] = jnp.zeros(halo_in.shape[1:], jnp.float32)
        face_halo[1] = jnp.zeros(face_halo.shape[1:], jnp.float32)

    @pl.when(jnp.logical_not(has_up))
    def _():
        face_in[...] = jnp.zeros(face_in.shape, jnp.float32)
        face_halo[...] = jnp.zeros(face_halo.shape, jnp.float32)

    acc[...] = jnp.zeros(acc.shape, jnp.float32)

    pl.semaphore_wait(barrier, expected)

    def par_copies(k):
        to = {"band": lax.rem(band + k, bands)}
        return (
            pltpu.make_async_remote_copy(
                src_ref=par_f.at[0],
                dst_ref=par_f.at[k],
                send_sem=par_send.at[0, k],
                recv_sem=par_recv.at[0, k],
                device_id=to,
                device_id_type=MESH,
            ),
            pltpu.make_async_remote_copy(
                src_ref=par_i.at[0],
                dst_ref=par_i.at[k],
                send_sem=par_send.at[1, k],
                recv_sem=par_recv.at[1, k],
                device_id=to,
                device_id_type=MESH,
            ),
        )

    for k in range(1, bands):
        for copy in par_copies(k):
            copy.start()

    for load in loads[:3]:
        load.wait()

    def spread(v):
        return jnp.where(own, v, half_turn(v))

    def prepare(zp, carry):
        packs = [[], []]
        for z in (zp, zp + pairs):
            for half in range(2):
                rows = pl.ds(half * ROWS, ROWS)
                o = spread(fields[0, z, rows])
                p = spread(fields[1, z, rows])
                levels = [spread(fields[2 + i, z, rows]) for i in range(LEVELS)]
                opac[z, half] = o
                plk[z, half] = p
                values = [o]
                for t in range(LINES):
                    low, up = levels[LOWER_LEVEL[t]], levels[UPPER_LEVEL[t]]
                    s = EPS_THERMAL * p + (1.0 - EPS_THERMAL) * (up / (low + up))
                    src[t, z, half] = s
                    values.append(s)
                packs[half].append(values)
        for i in range(1 + LINES):
            halo_out[0, zp, i] = jnp.where(left, packs[1][0][i], packs[1][1][i])
            halo_out[1, zp, i] = jnp.where(left, packs[0][1][i], packs[0][0][i])
        return carry

    lax.fori_loop(0, pairs, prepare, 0)

    def halo_copy(side):
        return pltpu.make_async_remote_copy(
            src_ref=halo_out.at[side],
            dst_ref=halo_in.at[side],
            send_sem=halo_send.at[side],
            recv_sem=halo_recv.at[side],
            device_id={"tile": tile + (1 if side == 0 else -1)},
            device_id_type=MESH,
        )

    @pl.when(has_right)
    def _():
        halo_copy(0).start()

    @pl.when(has_left)
    def _():
        halo_copy(1).start()

    for k in range(1, bands):
        for copy in par_copies(k):
            copy.wait_recv()
    to_scalars = pltpu.make_async_copy(par_i, par_s, idx_sem)
    to_scalars.start()
    to_scalars.wait()

    @pl.when(has_left)
    def _():
        halo_copy(0).wait_recv()

    @pl.when(has_right)
    def _():
        halo_copy(1).wait_recv()

    def unpack(zp, carry):
        for i in range(1 + LINES):
            a, b = halo_in[0, zp, i], halo_in[1, zp, i]
            first = jnp.where(left, a, b)
            second = half_turn(jnp.where(left, b, a))
            if i == 0:
                opac[zp, 2] = first
                opac[zp + pairs, 2] = second
            else:
                src[i - 1, zp, 2] = first
                src[i - 1, zp + pairs, 2] = second
        return carry

    lax.fori_loop(0, pairs, unpack, 0)

    def face_copies(chunk):
        def make(part, source, target, to):
            return pltpu.make_async_remote_copy(
                src_ref=source,
                dst_ref=target,
                send_sem=face_send.at[part, chunk],
                recv_sem=face_recv.at[part, chunk],
                device_id=to,
                device_id_type=MESH,
            )

        return (
            make(0, face_out.at[chunk], face_in.at[chunk], {"slab": slab + 1}),
            make(
                1,
                face_out.at[chunk, 1],
                face_halo.at[0, chunk],
                {"tile": tile + 1, "slab": slab + 1},
            ),
            make(
                2,
                face_out.at[chunk, 0],
                face_halo.at[1, chunk],
                {"tile": tile - 1, "slab": slab + 1},
            ),
        )

    def chunk_step(k, sub):
        chunk = k * subs + sub
        main, to_right, to_left = face_copies(chunk)

        @pl.when(has_up)
        def _():
            main.wait_recv()

        @pl.when(has_up & has_left)
        def _():
            to_right.wait_recv()

        @pl.when(has_up & has_right)
        def _():
            to_left.wait_recv()

        states, rates, weights, indices = [], [], [], []
        for f in range(BATCH):
            at = pl.ds(sub * BATCH + f, 1)
            rates.append(jnp.broadcast_to(par_f[k, 0, at], (ROWS, LANES)))
            w = jnp.broadcast_to(par_f[k, 1, at], (ROWS, LANES))
            t_of = jnp.broadcast_to(par_f[k, 2, at], (ROWS, LANES))
            weights.append([jnp.where(t_of == float(t), w, 0.0) for t in range(LINES)])
            indices.append(par_s[k, 0, sub * BATCH + f])
            beyond = jnp.where(left, face_halo[0, chunk, f], face_halo[1, chunk, f])
            states.append((face_in[chunk, 0, f], face_in[chunk, 1, f], beyond))
        for z in range(depth):
            last = z == depth - 1
            o = [opac[z, i] for i in range(2 if last else 3)]
            for f in range(BATCH):
                one, two, out = states[f]
                d1, d2, dh = (pltpu.roll(v, 1, 0) for v in (one, two, out))
                u1, u2, uh = (pltpu.roll(v, ROWS - 1, 0) for v in (one, two, out))
                winds = [
                    jnp.where(top_left, dh, jnp.where(low_right, u2, jnp.where(left, d1, u1))),
                    jnp.where(top_left, d1, jnp.where(low_right, uh, jnp.where(left, d2, u2))),
                    jnp.where(left, dh, uh),
                ]
                fresh = []
                for i in range(len(o)):
                    s = src[indices[f], z, i]
                    a = jnp.exp(rates[f] * o[i])
                    mixed = (1.0 - TILT_SHARE) * states[f][i] + TILT_SHARE * winds[i]
                    fresh.append(s + a * (mixed - s))
                if last:
                    fresh.append(out)
                states[f] = tuple(fresh)
            for half in range(2):
                for t in range(LINES):
                    total = acc[t, z, half]
                    for f in range(BATCH):
                        total = total + weights[f][t] * states[f][half]
                    acc[t, z, half] = total
        for f in range(BATCH):
            face_out[chunk, 0, f] = states[f][0]
            face_out[chunk, 1, f] = states[f][1]

        @pl.when(has_down)
        def _():
            main.start()

        @pl.when(has_down & has_right)
        def _():
            to_right.start()

        @pl.when(has_down & has_left)
        def _():
            to_left.start()

    def group_step(k, carry):
        for sub in range(subs):
            chunk_step(k, sub)
        return carry

    lax.fori_loop(0, bands, group_step, 0)

    def gather_copy(k, zp):
        return pltpu.make_async_remote_copy(
            src_ref=gathered.at[band, zp],
            dst_ref=gathered.at[band, zp],
            send_sem=gat_send.at[k, zp],
            recv_sem=gat_recv.at[k, zp],
            device_id={"band": lax.rem(band + k, bands)},
            device_id_type=MESH,
        )

    def arrival(k, zp):
        sender = lax.rem(band + bands - k, bands)
        return pltpu.make_async_remote_copy(
            src_ref=gathered.at[sender, zp],
            dst_ref=gathered.at[sender, zp],
            send_sem=gat_send.at[k, zp],
            recv_sem=gat_recv.at[k, zp],
            device_id={"band": lax.rem(band + k, bands)},
            device_id_type=MESH,
        )

    def relax(zp, carry):
        for half in range(2):
            both = []
            for z in (zp, zp + pairs):
                p = COLLISION * plk[z, half]
                ratios = []
                for t in range(LINES):
                    j = acc[t, z, half]
                    j = j + half_turn(j)
                    ratios.append((j + p) / ((1.0 + COLLISION) + j))
                one = 0.5 * (ratios[0] / ratios[2] + ratios[1] / ratios[3])
                levels = (one, ratios[1] / ratios[4], ratios[0], ratios[1])
                both.append(levels)
                scale = 1.0 / (1.0 + levels[0] + levels[1] + levels[2] + levels[3])
                rows = pl.ds(half * ROWS, ROWS)
                pops_out[0, z, rows] = scale[:, :HALF]
                for i in range(4):
                    pops_out[1 + i, z, rows] = (scale * levels[i])[:, :HALF]
            for i in range(4):
                gathered[band, zp, i, half] = jnp.where(left, both[0][i], both[1][i])
        for k in range(1, bands):
            gather_copy(k, zp).start()
        return carry

    lax.fori_loop(0, pairs, relax, 0)

    loads[3].wait()

    def finish(zp, carry):
        for k in range(1, bands):
            arrival(k, zp).wait_recv()
        for pair in range(bands // 2):
            columns = slice(pair * LANES, (pair + 1) * LANES)
            for half in range(2):
                rows = pl.ds(half * ROWS, ROWS)
                lines = []
                for b in (2 * pair, 2 * pair + 1):
                    levels = [1.0] + [gathered[b, zp, i, half] for i in range(4)]
                    lines.append(
                        [
                            levels[UPPER_LEVEL[t]] / (levels[LOWER_LEVEL[t]] + levels[UPPER_LEVEL[t]])
                            for t in range(LINES)
                        ]
                    )
                first = EPS_THERMAL * planck_all[zp, rows, columns]
                second = EPS_THERMAL * planck_all[zp + pairs, rows, columns]
                for t in range(LINES):
                    even, odd = lines[0][t], lines[1][t]
                    new_src[t, zp, rows, columns] = first + (1.0 - EPS_THERMAL) * jnp.where(
                        left, even, half_turn(odd)
                    )
                    new_src[t, zp + pairs, rows, columns] = second + (
                        1.0 - EPS_THERMAL
                    ) * jnp.where(left, half_turn(even), odd)
        for f in range(freqs):
            t = line_index[f]
            source_out[f, zp] = new_src[t, zp]
            source_out[f, zp + pairs] = new_src[t, zp + pairs]
        return carry

    lax.fori_loop(0, pairs, finish, 0)

    for k in range(1, bands):
        for copy in par_copies(k):
            copy.wait_send()

    @pl.when(has_right)
    def _():
        halo_copy(0).wait_send()

    @pl.when(has_left)
    def _():
        halo_copy(1).wait_send()

    def drain(chunk, carry):
        main, to_right, to_left = face_copies(chunk)

        @pl.when(has_down)
        def _():
            main.wait_send()

        @pl.when(has_down & has_right)
        def _():
            to_right.wait_send()

        @pl.when(has_down & has_left)
        def _():
            to_left.wait_send()

        return carry

    lax.fori_loop(0, bands * subs, drain, 0)

    def drain_gather(zp, carry):
        for k in range(1, bands):
            gather_copy(k, zp).wait_send()
        return carry

    lax.fori_loop(0, pairs, drain_gather, 0)


def per_device(sizes, strength, opacity, planck, old_populations, line_index, line_weight):
    bands, tiles, slabs = sizes
    depth, rows, cells = opacity.shape
    freqs = strength.shape[0]
    pairs = depth // 2
    chunks = bands * freqs // BATCH
    assert rows == 2 * ROWS and depth <= ROWS and cells == bands * HALF
    f32 = jnp.float32
    scalars = pl.BlockSpec(memory_space=pltpu.SMEM)
    anywhere = pl.BlockSpec(memory_space=pl.ANY)
    vmem = pl.BlockSpec(memory_space=pltpu.VMEM)
    sem = pltpu.SemaphoreType.DMA
    tile = (ROWS, LANES)
    return pl.pallas_call(
        functools.partial(kernel, (bands, tiles, slabs, depth, freqs)),
        out_shape=(
            jax.ShapeDtypeStruct((LEVELS, depth, rows, cells // bands), f32),
            jax.ShapeDtypeStruct((freqs, depth, rows, cells), f32),
        ),
        in_specs=[scalars] * 3 + [anywhere] * 3,
        out_specs=(vmem, vmem),
        scratch_shapes=[
            pltpu.VMEM((2 + LEVELS, depth, rows, LANES), f32),
            pltpu.VMEM((depth, rows, cells), f32),
            pltpu.VMEM((bands, 3) + tile, f32),
            pltpu.VMEM((bands, 1, LANES), jnp.int32),
            pltpu.SMEM((bands, 1, LANES), jnp.int32),
            pltpu.VMEM((2, pairs, 1 + LINES) + tile, f32),
            pltpu.VMEM((2, pairs, 1 + LINES) + tile, f32),
            pltpu.VMEM((depth, 3) + tile, f32),
            pltpu.VMEM((LINES, depth, 3) + tile, f32),
            pltpu.VMEM((depth, 2) + tile, f32),
            pltpu.VMEM((chunks, 2, BATCH) + tile, f32),
            pltpu.VMEM((2, chunks, BATCH) + tile, f32),
            pltpu.VMEM((chunks, 2, BATCH) + tile, f32),
            pltpu.VMEM((LINES, depth, 2) + tile, f32),
            pltpu.VMEM((bands, pairs, 4, 2) + tile, f32),
            pltpu.VMEM((LINES, depth, rows, cells), f32),
            sem((4,)),
            sem,
            sem((2, bands)),
            sem((2, bands)),
            sem((2,)),
            sem((2,)),
            sem((3, chunks)),
            sem((3, chunks)),
            sem((bands, pairs)),
            sem((bands, pairs)),
        ],
        compiler_params=pltpu.CompilerParams(
            collective_id=0, has_side_effects=True, vmem_limit_bytes=32 * 1024 * 1024
        ),
        cost_estimate=pl.CostEstimate(
            flops=60 * depth * rows * cells * freqs,
            bytes_accessed=16 * depth * rows * cells * 4,
            transcendentals=2 * depth * rows * cells * freqs,
        ),
    )(strength, line_index, line_weight, opacity, planck, old_populations)


def solution(mesh):
    sizes = (mesh.shape["band"], mesh.shape["tile"], mesh.shape["slab"])
    in_specs = (
        P("band"),
        P("slab", "tile", None),
        P("slab", "tile", None),
        P(None, "slab", "tile", None),
        P("band"),
        P("band"),
    )
    out_specs = (P(None, "slab", "tile", "band"), P("band", "slab", "tile", None))
    return jax.shard_map(
        functools.partial(per_device, sizes),
        mesh=mesh,
        in_specs=in_specs,
        out_specs=out_specs,
        check_vma=False,
    )
```

```python
import functools

import jax
import jax.numpy as jnp
from jax import lax
from jax.experimental import pallas as pl
from jax.experimental.pallas import tpu as pltpu
from jax.sharding import PartitionSpec as P

MESH = pl.DeviceIdType.MESH
LINES = 5
LEVELS = 5
EPS_THERMAL = 0.1
COLLISION = 0.5
PATH_FACTOR = 1.25
TILT_SHARE = 0.4
LOWER_LEVEL = (0, 0, 1, 1, 2)
UPPER_LEVEL = (3, 4, 3, 4, 4)
LANES = 128
ROWS = 8
HALF = LANES // 2
BATCH = 4


def half_turn(v):
    return pltpu.roll(v, HALF, 1)


def kernel(
    sizes,
    strength_hbm,
    line_index_hbm,
    line_weight_hbm,
    opacity,
    planck,
    populations,
    pops_out,
    source_out,
    strength,
    line_index,
    line_weight,
    fields,
    planck_all,
    par_f,
    par_i,
    par_s,
    halo_out,
    halo_in,
    opac,
    src,
    plk,
    face_in,
    face_halo,
    face_out,
    acc,
    gathered,
    new_src,
    in_sem,
    idx_sem,
    par_send,
    par_recv,
    halo_send,
    halo_recv,
    face_send,
    face_recv,
    gat_send,
    gat_recv,
):
    bands, tiles, slabs, depth, freqs = sizes
    pairs = depth // 2
    subs = freqs // BATCH
    band = lax.axis_index("band")
    tile = lax.axis_index("tile")
    slab = lax.axis_index("slab")
    has_left = tile > 0
    has_right = tile < tiles - 1
    has_up = slab > 0
    has_down = slab < slabs - 1

    column = pl.multiple_of((band // 2) * LANES, LANES)
    loads = [
        pltpu.make_async_copy(opacity.at[:, :, pl.ds(column, LANES)], fields.at[0], in_sem.at[0]),
        pltpu.make_async_copy(planck.at[:, :, pl.ds(column, LANES)], fields.at[1], in_sem.at[1]),
        pltpu.make_async_copy(
            populations.at[:, :, :, pl.ds(column, LANES)], fields.at[pl.ds(2, LEVELS)], in_sem.at[2]
        ),
        pltpu.make_async_copy(strength_hbm, strength, in_sem.at[3]),
        pltpu.make_async_copy(line_index_hbm, line_index, in_sem.at[4]),
        pltpu.make_async_copy(line_weight_hbm, line_weight, in_sem.at[5]),
        pltpu.make_async_copy(planck, planck_all, in_sem.at[6]),
    ]
    for load in loads:
        load.start()

    barrier = pltpu.get_barrier_semaphore()
    for k in range(1, bands):
        pl.semaphore_signal(
            barrier, inc=1, device_id={"band": lax.rem(band + k, bands)}, device_id_type=MESH
        )
    expected = jnp.int32(bands - 1)
    for dt in (-1, 0, 1):
        for ds in (-1, 0, 1):
            if dt == 0 and ds == 0:
                continue
            there = (tile + dt >= 0) & (tile + dt < tiles) & (slab + ds >= 0) & (slab + ds < slabs)

            @pl.when(there)
            def _():
                pl.semaphore_signal(
                    barrier,
                    inc=1,
                    device_id={"tile": tile + dt, "slab": slab + ds},
                    device_id_type=MESH,
                )

            expected = expected + there.astype(jnp.int32)

    row = lax.broadcasted_iota(jnp.int32, (ROWS, LANES), 0)
    lane = lax.broadcasted_iota(jnp.int32, (ROWS, LANES), 1)
    left = lane < HALF
    own = (lane // HALF) == lax.rem(band, 2)
    top_left = left & (row == 0)
    low_right = jnp.logical_not(left) & (row == ROWS - 1)

    @pl.when(jnp.logical_not(has_left))
    def _():
        halo_in[0] = jnp.zeros(halo_in.shape[1:], jnp.float32)
        face_halo[0] = jnp.zeros(face_halo.shape[1:], jnp.float32)

    @pl.when(jnp.logical_not(has_right))
    def _():
        halo_in[1] = jnp.zeros(halo_in.shape[1:], jnp.float32)
        face_halo[1] = jnp.zeros(face_halo.shape[1:], jnp.float32)

    @pl.when(jnp.logical_not(has_up))
    def _():
        face_in[...] = jnp.zeros(face_in.shape, jnp.float32)
        face_halo[...] = jnp.zeros(face_halo.shape, jnp.float32)

    acc[...] = jnp.zeros(acc.shape, jnp.float32)

    def par_copies(k):
        to = {"band": lax.rem(band + k, bands)}
        return (
            pltpu.make_async_remote_copy(
                src_ref=par_f.at[0],
                dst_ref=par_f.at[k],
                send_sem=par_send.at[0, k],
                recv_sem=par_recv.at[0, k],
                device_id=to,
                device_id_type=MESH,
            ),
            pltpu.make_async_remote_copy(
                src_ref=par_i.at[0],
                dst_ref=par_i.at[k],
                send_sem=par_send.at[1, k],
                recv_sem=par_recv.at[1, k],
                device_id=to,
                device_id_type=MESH,
            ),
        )

    for load in loads[:6]:
        load.wait()

    lane_row = lax.broadcasted_iota(jnp.int32, (1, LANES), 1)
    indices = jnp.zeros((1, LANES), jnp.int32)
    zero = jnp.zeros((ROWS, LANES), jnp.float32)
    rate, weight, which = zero, zero, zero
    for f in range(freqs):
        here = row == f
        rate = jnp.where(here, -PATH_FACTOR * strength[f], rate)
        weight = jnp.where(here, line_weight[f] * (LINES / (2.0 * freqs * bands)), weight)
        which = jnp.where(here, line_index[f].astype(jnp.float32), which)
        indices = jnp.where(lane_row == f, line_index[f], indices)
    par_f[0, 0] = rate
    par_f[0, 1] = weight
    par_f[0, 2] = which
    par_i[0] = indices

    def spread(v):
        return jnp.where(own, v, half_turn(v))

    def prepare(z, carry):
        for half in range(2):
            rows = pl.ds(half * ROWS, ROWS)
            p = spread(fields[1, z, rows])
            levels = [spread(fields[2 + i, z, rows]) for i in range(LEVELS)]
            opac[z, half] = spread(fields[0, z, rows])
            plk[z, half] = p
            for t in range(LINES):
                low, up = levels[LOWER_LEVEL[t]], levels[UPPER_LEVEL[t]]
                src[t, z, half] = EPS_THERMAL * p + (1.0 - EPS_THERMAL) * (up / (low + up))
        return carry

    lax.fori_loop(0, depth, prepare, 0)

    def layer(i, z, part):
        return opac[z, part] if i == 0 else src[i - 1, z, part]

    for i in range(1 + LINES):
        right, down = [], []
        for z in range(pairs):
            y = depth - 2 - z
            a, b = layer(i, z, 1), layer(i, z, 0)
            if y > z:
                a = jnp.where(row >= 1 + z, a, pltpu.roll(layer(i, y, 1), z + 1, 0))
                b = jnp.where(row <= y, b, pltpu.roll(layer(i, y, 0), y + 1, 0))
            right.append(a)
            down.append(b)
        for q in range(pairs // 2):
            halo_out[0, i, q] = jnp.where(left, right[q], right[q + pairs // 2])
            halo_out[1, i, q] = jnp.where(left, down[q + pairs // 2], down[q])

    pl.semaphore_wait(barrier, expected)
    for k in range(1, bands):
        for copy in par_copies(k):
            copy.start()

    def halo_copy(side):
        return pltpu.make_async_remote_copy(
            src_ref=halo_out.at[side],
            dst_ref=halo_in.at[side],
            send_sem=halo_send.at[side],
            recv_sem=halo_recv.at[side],
            device_id={"tile": tile + (1 if side == 0 else -1)},
            device_id_type=MESH,
        )

    @pl.when(has_right)
    def _():
        halo_copy(0).start()

    @pl.when(has_left)
    def _():
        halo_copy(1).start()

    for k in range(1, bands):
        for copy in par_copies(k):
            copy.wait_recv()
    to_scalars = pltpu.make_async_copy(par_i, par_s, idx_sem)
    to_scalars.start()
    to_scalars.wait()

    @pl.when(has_left)
    def _():
        halo_copy(0).wait_recv()

    @pl.when(has_right)
    def _():
        halo_copy(1).wait_recv()

    for i in range(1 + LINES):
        for q in range(pairs // 2):
            a, b = halo_in[0, i, q], halo_in[1, i, q]
            shared = {q: jnp.where(left, a, b)}
            shared[q + pairs // 2] = half_turn(jnp.where(left, b, a))
            for z, tile_rows in shared.items():
                y = depth - 2 - z
                both = [(z, tile_rows)]
                if y > z:
                    moved = (pltpu.roll(tile_rows, y + 1, 0), pltpu.roll(tile_rows, z + 1, 0))
                    both.append((y, jnp.where(left, *moved)))
                for at, v in both:
                    if i == 0:
                        opac[at, 2] = v
                    else:
                        src[i - 1, at, 2] = v

    def face_copies(chunk):
        def make(part, source, target, to):
            return pltpu.make_async_remote_copy(
                src_ref=source,
                dst_ref=target,
                send_sem=face_send.at[part, chunk],
                recv_sem=face_recv.at[part, chunk],
                device_id=to,
                device_id_type=MESH,
            )

        return (
            make(0, face_out.at[chunk], face_in.at[chunk], {"slab": slab + 1}),
            make(
                1,
                face_out.at[chunk, 1],
                face_halo.at[0, chunk],
                {"tile": tile + 1, "slab": slab + 1},
            ),
            make(
                2,
                face_out.at[chunk, 0],
                face_halo.at[1, chunk],
                {"tile": tile - 1, "slab": slab + 1},
            ),
        )

    def chunk_step(k, sub):
        chunk = k * subs + sub
        main, to_right, to_left = face_copies(chunk)

        @pl.when(has_up)
        def _():
            main.wait_recv()

        @pl.when(has_up & has_left)
        def _():
            to_right.wait_recv()

        @pl.when(has_up & has_right)
        def _():
            to_left.wait_recv()

        states, rates, weights, indices = [], [], [], []
        for f in range(BATCH):
            at = pl.ds(sub * BATCH + f, 1)
            rates.append(jnp.broadcast_to(par_f[k, 0, at], (ROWS, LANES)))
            w = jnp.broadcast_to(par_f[k, 1, at], (ROWS, LANES))
            t_of = jnp.broadcast_to(par_f[k, 2, at], (ROWS, LANES))
            weights.append([jnp.where(t_of == float(t), w, 0.0) for t in range(LINES)])
            indices.append(par_s[k, 0, sub * BATCH + f])
            beyond = jnp.where(left, face_halo[0, chunk, f], face_halo[1, chunk, f])
            states.append((face_in[chunk, 0, f], face_in[chunk, 1, f], beyond))
        for z in range(depth):
            last = z == depth - 1
            o = [opac[z, i] for i in range(2 if last else 3)]
            for f in range(BATCH):
                one, two, out = states[f]
                d1, d2, dh = (pltpu.roll(v, 1, 0) for v in (one, two, out))
                u1, u2, uh = (pltpu.roll(v, ROWS - 1, 0) for v in (one, two, out))
                winds = [
                    jnp.where(top_left, dh, jnp.where(low_right, u2, jnp.where(left, d1, u1))),
                    jnp.where(top_left, d1, jnp.where(low_right, uh, jnp.where(left, d2, u2))),
                    jnp.where(left, dh, uh),
                ]
                fresh = []
                for i in range(len(o)):
                    s = src[indices[f], z, i]
                    a = jnp.exp(rates[f] * o[i])
                    mixed = (1.0 - TILT_SHARE) * states[f][i] + TILT_SHARE * winds[i]
                    fresh.append(s + a * (mixed - s))
                if last:
                    fresh.append(out)
                states[f] = tuple(fresh)
            for half in range(2):
                for t in range(LINES):
                    total = acc[t, z, half]
                    for f in range(BATCH):
                        total = total + weights[f][t] * states[f][half]
                    acc[t, z, half] = total
        for f in range(BATCH):
            face_out[chunk, 0, f] = states[f][0]
            face_out[chunk, 1, f] = states[f][1]

        @pl.when(has_down)
        def _():
            main.start()

        @pl.when(has_down & has_right)
        def _():
            to_right.start()

        @pl.when(has_down & has_left)
        def _():
            to_left.start()

    def group_step(k, carry):
        for sub in range(subs):
            chunk_step(k, sub)
        return carry

    lax.fori_loop(0, bands, group_step, 0)

    beside = band + 1 - 2 * lax.rem(band, 2)
    across = lax.rem(band + 2, bands)
    corner = bands - 1 - band

    def gather_copy(kind, owner, zp, to):
        return pltpu.make_async_remote_copy(
            src_ref=gathered.at[owner, zp],
            dst_ref=gathered.at[owner, zp],
            send_sem=gat_send.at[kind, zp],
            recv_sem=gat_recv.at[kind, zp],
            device_id={"band": to},
            device_id_type=MESH,
        )

    def relax(zp, carry):
        for half in range(2):
            both = []
            for z in (zp, zp + pairs):
                p = COLLISION * plk[z, half]
                ratios = []
                for t in range(LINES):
                    j = acc[t, z, half]
                    j = j + half_turn(j)
                    ratios.append((j + p) / ((1.0 + COLLISION) + j))
                one = 0.5 * (ratios[0] / ratios[2] + ratios[1] / ratios[3])
                levels = (one, ratios[1] / ratios[4], ratios[0], ratios[1])
                both.append(levels)
                scale = 1.0 / (1.0 + levels[0] + levels[1] + levels[2] + levels[3])
                rows = pl.ds(half * ROWS, ROWS)
                pops_out[0, z, rows] = scale[:, :HALF]
                for i in range(4):
                    pops_out[1 + i, z, rows] = (scale * levels[i])[:, :HALF]
            for i in range(4):
                gathered[band, zp, i, half] = jnp.where(left, both[0][i], both[1][i])
        gather_copy(0, band, zp, beside).start()
        gather_copy(1, band, zp, across).start()
        return carry

    lax.fori_loop(0, pairs, relax, 0)

    loads[6].wait()

    def forward(q, carry):
        gather_copy(0, beside, 2 * q, beside).wait_recv()
        gather_copy(2, beside, 2 * q, across).start()
        gather_copy(1, across, 2 * q + 1, across).wait_recv()
        gather_copy(2, across, 2 * q + 1, beside).start()
        return carry

    lax.fori_loop(0, pairs // 2, forward, 0)

    def finish_two(q, carry):
        gather_copy(1, across, 2 * q, across).wait_recv()
        gather_copy(2, corner, 2 * q, corner).wait_recv()
        finish(2 * q)
        gather_copy(0, beside, 2 * q + 1, beside).wait_recv()
        gather_copy(2, corner, 2 * q + 1, corner).wait_recv()
        finish(2 * q + 1)
        return carry

    def finish(zp):
        for pair in range(bands // 2):
            columns = slice(pair * LANES, (pair + 1) * LANES)
            for half in range(2):
                rows = pl.ds(half * ROWS, ROWS)
                lines = []
                for b in (2 * pair, 2 * pair + 1):
                    levels = [1.0] + [gathered[b, zp, i, half] for i in range(4)]
                    lines.append(
                        [
                            levels[UPPER_LEVEL[t]] / (levels[LOWER_LEVEL[t]] + levels[UPPER_LEVEL[t]])
                            for t in range(LINES)
                        ]
                    )
                first = EPS_THERMAL * planck_all[zp, rows, columns]
                second = EPS_THERMAL * planck_all[zp + pairs, rows, columns]
                for t in range(LINES):
                    even, odd = lines[0][t], lines[1][t]
                    new_src[t, zp, rows, columns] = first + (1.0 - EPS_THERMAL) * jnp.where(
                        left, even, half_turn(odd)
                    )
                    new_src[t, zp + pairs, rows, columns] = second + (
                        1.0 - EPS_THERMAL
                    ) * jnp.where(left, half_turn(even), odd)
        for f in range(freqs):
            t = line_index[f]
            source_out[f, zp] = new_src[t, zp]
            source_out[f, zp + pairs] = new_src[t, zp + pairs]

    lax.fori_loop(0, pairs // 2, finish_two, 0)

    for k in range(1, bands):
        for copy in par_copies(k):
            copy.wait_send()

    @pl.when(has_right)
    def _():
        halo_copy(0).wait_send()

    @pl.when(has_left)
    def _():
        halo_copy(1).wait_send()

    def drain(chunk, carry):
        main, to_right, to_left = face_copies(chunk)

        @pl.when(has_down)
        def _():
            main.wait_send()

        @pl.when(has_down & has_right)
        def _():
            to_right.wait_send()

        @pl.when(has_down & has_left)
        def _():
            to_left.wait_send()

        return carry

    lax.fori_loop(0, bands * subs, drain, 0)

    def drain_gather(zp, carry):
        gather_copy(0, band, zp, beside).wait_send()
        gather_copy(1, band, zp, across).wait_send()
        gather_copy(2, corner, zp, across).wait_send()
        return carry

    lax.fori_loop(0, pairs, drain_gather, 0)


def write_out(pops, source, pops_hbm, source_hbm, sem):
    copies = [pltpu.make_async_copy(pops, pops_hbm, sem.at[0])]
    for f in range(source.shape[0]):
        copies.append(pltpu.make_async_copy(source.at[f], source_hbm.at[f], sem.at[1 + f]))
    for copy in copies:
        copy.start()
    for copy in copies:
        copy.wait()


def per_device(sizes, strength, opacity, planck, old_populations, line_index, line_weight):
    bands, tiles, slabs = sizes
    depth, rows, cells = opacity.shape
    freqs = strength.shape[0]
    pairs = depth // 2
    chunks = bands * freqs // BATCH
    assert rows == 2 * ROWS and depth == ROWS and cells == bands * HALF and bands == 4
    f32 = jnp.float32
    hbm = pl.BlockSpec(memory_space=pltpu.HBM)
    anywhere = pl.BlockSpec(memory_space=pl.ANY)
    vmem = pl.BlockSpec(memory_space=pltpu.VMEM)
    sem = pltpu.SemaphoreType.DMA
    tile = (ROWS, LANES)
    pops, source = pl.pallas_call(
        functools.partial(kernel, (bands, tiles, slabs, depth, freqs)),
        out_shape=(
            jax.ShapeDtypeStruct((LEVELS, depth, rows, cells // bands), f32),
            jax.ShapeDtypeStruct((freqs, depth, rows, cells), f32),
        ),
        in_specs=[hbm] * 6,
        out_specs=(vmem, vmem),
        scratch_shapes=[
            pltpu.SMEM((freqs,), f32),
            pltpu.SMEM((freqs,), jnp.int32),
            pltpu.SMEM((freqs,), f32),
            pltpu.VMEM((2 + LEVELS, depth, rows, LANES), f32),
            pltpu.VMEM((depth, rows, cells), f32),
            pltpu.VMEM((bands, 3) + tile, f32),
            pltpu.VMEM((bands, 1, LANES), jnp.int32),
            pltpu.SMEM((bands, 1, LANES), jnp.int32),
            pltpu.VMEM((2, 1 + LINES, pairs // 2) + tile, f32),
            pltpu.VMEM((2, 1 + LINES, pairs // 2) + tile, f32),
            pltpu.VMEM((depth, 3) + tile, f32),
            pltpu.VMEM((LINES, depth, 3) + tile, f32),
            pltpu.VMEM((depth, 2) + tile, f32),
            pltpu.VMEM((chunks, 2, BATCH) + tile, f32),
            pltpu.VMEM((2, chunks, BATCH) + tile, f32),
            pltpu.VMEM((chunks, 2, BATCH) + tile, f32),
            pltpu.VMEM((LINES, depth, 2) + tile, f32),
            pltpu.VMEM((bands, pairs, 4, 2) + tile, f32),
            pltpu.VMEM((LINES, depth, rows, cells), f32),
            sem((7,)),
            sem,
            sem((2, bands)),
            sem((2, bands)),
            sem((2,)),
            sem((2,)),
            sem((3, chunks)),
            sem((3, chunks)),
            sem((3, pairs)),
            sem((3, pairs)),
        ],
        compiler_params=pltpu.CompilerParams(
            collective_id=0, has_side_effects=True, vmem_limit_bytes=32 * 1024 * 1024
        ),
        cost_estimate=pl.CostEstimate(
            flops=60 * depth * rows * cells * freqs,
            bytes_accessed=16 * depth * rows * cells * 4,
            transcendentals=2 * depth * rows * cells * freqs,
        ),
    )(
        *(
            pltpu.with_memory_space_constraint(v, pltpu.HBM)
            for v in (strength, line_index, line_weight, opacity, planck, old_populations)
        )
    )
    return pl.pallas_call(
        write_out,
        out_shape=(
            jax.ShapeDtypeStruct(pops.shape, f32),
            jax.ShapeDtypeStruct(source.shape, f32),
        ),
        in_specs=[anywhere] * 2,
        out_specs=(hbm, hbm),
        scratch_shapes=[sem((1 + freqs,))],
    )(pops, source)


def solution(mesh):
    sizes = (mesh.shape["band"], mesh.shape["tile"], mesh.shape["slab"])
    in_specs = (
        P("band"),
        P("slab", "tile", None),
        P("slab", "tile", None),
        P(None, "slab", "tile", None),
        P("band"),
        P("band"),
    )
    out_specs = (P(None, "slab", "tile", "band"), P("band", "slab", "tile", None))
    return jax.shard_map(
        functools.partial(per_device, sizes),
        mesh=mesh,
        in_specs=in_specs,
        out_specs=out_specs,
        check_vma=False,
    )
```

```python
import functools

import jax
import jax.numpy as jnp
from jax import lax
from jax.experimental import pallas as pl
from jax.experimental.pallas import tpu as pltpu
from jax.sharding import PartitionSpec as P

MESH = pl.DeviceIdType.MESH
LINES = 5
LEVELS = 5
EPS_THERMAL = 0.1
COLLISION = 0.5
PATH_FACTOR = 1.25
TILT_SHARE = 0.4
LOWER_LEVEL = (0, 0, 1, 1, 2)
UPPER_LEVEL = (3, 4, 3, 4, 4)
LANES = 128
ROWS = 8
HALF = LANES // 2
BATCH = 4


def half_turn(v):
    return pltpu.roll(v, HALF, 1)


def kernel(
    sizes,
    strength_hbm,
    line_index_hbm,
    line_weight_hbm,
    opacity,
    planck,
    populations,
    pops_out,
    source_out,
    strength,
    line_index,
    line_weight,
    fields,
    planck_all,
    par_f,
    par_i,
    par_s,
    halo_out,
    halo_in,
    opac,
    src,
    plk,
    face_in,
    face_halo,
    face_out,
    acc,
    gathered,
    new_src,
    in_sem,
    idx_sem,
    par_send,
    par_recv,
    halo_send,
    halo_recv,
    face_send,
    face_recv,
    gat_send,
    gat_recv,
):
    bands, tiles, slabs, depth, freqs = sizes
    pairs = depth // 2
    subs = freqs // BATCH
    band = lax.axis_index("band")
    tile = lax.axis_index("tile")
    slab = lax.axis_index("slab")
    has_left = tile > 0
    has_right = tile < tiles - 1
    has_up = slab > 0
    has_down = slab < slabs - 1

    column = pl.multiple_of((band // 2) * LANES, LANES)
    loads = [
        pltpu.make_async_copy(opacity.at[:, :, pl.ds(column, LANES)], fields.at[0], in_sem.at[0]),
        pltpu.make_async_copy(planck.at[:, :, pl.ds(column, LANES)], fields.at[1], in_sem.at[1]),
        pltpu.make_async_copy(
            populations.at[:, :, :, pl.ds(column, LANES)], fields.at[pl.ds(2, LEVELS)], in_sem.at[2]
        ),
        pltpu.make_async_copy(strength_hbm, strength, in_sem.at[3]),
        pltpu.make_async_copy(line_index_hbm, line_index, in_sem.at[4]),
        pltpu.make_async_copy(line_weight_hbm, line_weight, in_sem.at[5]),
        pltpu.make_async_copy(planck, planck_all, in_sem.at[6]),
    ]
    for load in loads:
        load.start()

    barrier = pltpu.get_barrier_semaphore()
    for k in range(1, bands):
        pl.semaphore_signal(
            barrier, inc=1, device_id={"band": lax.rem(band + k, bands)}, device_id_type=MESH
        )
    expected = jnp.int32(bands - 1)
    for dt in (-1, 0, 1):
        for ds in (-1, 0, 1):
            if dt == 0 and ds == 0:
                continue
            there = (tile + dt >= 0) & (tile + dt < tiles) & (slab + ds >= 0) & (slab + ds < slabs)

            @pl.when(there)
            def _():
                pl.semaphore_signal(
                    barrier,
                    inc=1,
                    device_id={"tile": tile + dt, "slab": slab + ds},
                    device_id_type=MESH,
                )

            expected = expected + there.astype(jnp.int32)

    row = lax.broadcasted_iota(jnp.int32, (ROWS, LANES), 0)
    lane = lax.broadcasted_iota(jnp.int32, (ROWS, LANES), 1)
    left = lane < HALF
    own = (lane // HALF) == lax.rem(band, 2)
    top_left = left & (row == 0)
    low_right = jnp.logical_not(left) & (row == ROWS - 1)

    @pl.when(jnp.logical_not(has_left))
    def _():
        halo_in[0] = jnp.zeros(halo_in.shape[1:], jnp.float32)
        face_halo[0] = jnp.zeros(face_halo.shape[1:], jnp.float32)

    @pl.when(jnp.logical_not(has_right))
    def _():
        halo_in[1] = jnp.zeros(halo_in.shape[1:], jnp.float32)
        face_halo[1] = jnp.zeros(face_halo.shape[1:], jnp.float32)

    @pl.when(jnp.logical_not(has_up))
    def _():
        face_in[...] = jnp.zeros(face_in.shape, jnp.float32)
        face_halo[...] = jnp.zeros(face_halo.shape, jnp.float32)

    acc[...] = jnp.zeros(acc.shape, jnp.float32)

    def par_copies(k):
        to = {"band": lax.rem(band + k, bands)}
        return (
            pltpu.make_async_remote_copy(
                src_ref=par_f.at[0],
                dst_ref=par_f.at[k],
                send_sem=par_send.at[0, k],
                recv_sem=par_recv.at[0, k],
                device_id=to,
                device_id_type=MESH,
            ),
            pltpu.make_async_remote_copy(
                src_ref=par_i.at[0],
                dst_ref=par_i.at[k],
                send_sem=par_send.at[1, k],
                recv_sem=par_recv.at[1, k],
                device_id=to,
                device_id_type=MESH,
            ),
        )

    for load in loads[:6]:
        load.wait()

    lane_row = lax.broadcasted_iota(jnp.int32, (1, LANES), 1)
    indices = jnp.zeros((1, LANES), jnp.int32)
    zero = jnp.zeros((ROWS, LANES), jnp.float32)
    rate, weight, which = zero, zero, zero
    for f in range(freqs):
        here = row == f
        rate = jnp.where(here, -PATH_FACTOR * strength[f], rate)
        weight = jnp.where(here, line_weight[f] * (LINES / (2.0 * freqs * bands)), weight)
        which = jnp.where(here, line_index[f].astype(jnp.float32), which)
        indices = jnp.where(lane_row == f, line_index[f], indices)
    par_f[0, 0] = rate
    par_f[0, 1] = weight
    par_f[0, 2] = which
    par_i[0] = indices

    def spread(v):
        return jnp.where(own, v, half_turn(v))

    def prepare(z, carry):
        for half in range(2):
            rows = pl.ds(half * ROWS, ROWS)
            p = spread(fields[1, z, rows])
            levels = [spread(fields[2 + i, z, rows]) for i in range(LEVELS)]
            opac[z, half] = spread(fields[0, z, rows])
            plk[z, half] = p
            for t in range(LINES):
                low, up = levels[LOWER_LEVEL[t]], levels[UPPER_LEVEL[t]]
                src[t, z, half] = EPS_THERMAL * p + (1.0 - EPS_THERMAL) * (up / (low + up))
        return carry

    lax.fori_loop(0, depth, prepare, 0)

    def layer(i, z, part):
        return opac[z, part] if i == 0 else src[i - 1, z, part]

    for i in range(1 + LINES):
        right, down = [], []
        for z in range(pairs):
            y = depth - 2 - z
            a, b = layer(i, z, 1), layer(i, z, 0)
            if y > z:
                a = jnp.where(row >= 1 + z, a, pltpu.roll(layer(i, y, 1), z + 1, 0))
                b = jnp.where(row <= y, b, pltpu.roll(layer(i, y, 0), y + 1, 0))
            right.append(a)
            down.append(b)
        for q in range(pairs // 2):
            halo_out[0, i, q] = jnp.where(left, right[q], right[q + pairs // 2])
            halo_out[1, i, q] = jnp.where(left, down[q + pairs // 2], down[q])

    pl.semaphore_wait(barrier, expected)
    for k in range(1, bands):
        for copy in par_copies(k):
            copy.start()

    def halo_copy(side):
        return pltpu.make_async_remote_copy(
            src_ref=halo_out.at[side],
            dst_ref=halo_in.at[side],
            send_sem=halo_send.at[side],
            recv_sem=halo_recv.at[side],
            device_id={"tile": tile + (1 if side == 0 else -1)},
            device_id_type=MESH,
        )

    @pl.when(has_right)
    def _():
        halo_copy(0).start()

    @pl.when(has_left)
    def _():
        halo_copy(1).start()

    for k in range(1, bands):
        for copy in par_copies(k):
            copy.wait_recv()
    to_scalars = pltpu.make_async_copy(par_i, par_s, idx_sem)
    to_scalars.start()
    to_scalars.wait()

    @pl.when(has_left)
    def _():
        halo_copy(0).wait_recv()

    @pl.when(has_right)
    def _():
        halo_copy(1).wait_recv()

    for i in range(1 + LINES):
        for q in range(pairs // 2):
            a, b = halo_in[0, i, q], halo_in[1, i, q]
            shared = {q: jnp.where(left, a, b)}
            shared[q + pairs // 2] = half_turn(jnp.where(left, b, a))
            for z, tile_rows in shared.items():
                y = depth - 2 - z
                both = [(z, tile_rows)]
                if y > z:
                    moved = (pltpu.roll(tile_rows, y + 1, 0), pltpu.roll(tile_rows, z + 1, 0))
                    both.append((y, jnp.where(left, *moved)))
                for at, v in both:
                    if i == 0:
                        opac[at, 2] = v
                    else:
                        src[i - 1, at, 2] = v

    def face_copies(chunk):
        def make(part, source, target, to):
            return pltpu.make_async_remote_copy(
                src_ref=source,
                dst_ref=target,
                send_sem=face_send.at[part, chunk],
                recv_sem=face_recv.at[part, chunk],
                device_id=to,
                device_id_type=MESH,
            )

        return (
            make(0, face_out.at[chunk], face_in.at[chunk], {"slab": slab + 1}),
            make(
                1,
                face_out.at[chunk, 1],
                face_halo.at[0, chunk],
                {"tile": tile + 1, "slab": slab + 1},
            ),
            make(
                2,
                face_out.at[chunk, 0],
                face_halo.at[1, chunk],
                {"tile": tile - 1, "slab": slab + 1},
            ),
        )

    def chunk_step(k, sub):
        chunk = k * subs + sub
        main, to_right, to_left = face_copies(chunk)

        @pl.when(has_up)
        def _():
            main.wait_recv()

        @pl.when(has_up & has_left)
        def _():
            to_right.wait_recv()

        @pl.when(has_up & has_right)
        def _():
            to_left.wait_recv()

        states, rates, weights, indices = [], [], [], []
        for f in range(BATCH):
            at = pl.ds(sub * BATCH + f, 1)
            rates.append(jnp.broadcast_to(par_f[k, 0, at], (ROWS, LANES)))
            w = jnp.broadcast_to(par_f[k, 1, at], (ROWS, LANES))
            t_of = jnp.broadcast_to(par_f[k, 2, at], (ROWS, LANES))
            weights.append([jnp.where(t_of == float(t), w, 0.0) for t in range(LINES)])
            indices.append(par_s[k, 0, sub * BATCH + f])
            beyond = jnp.where(left, face_halo[0, chunk, f], face_halo[1, chunk, f])
            states.append((face_in[chunk, 0, f], face_in[chunk, 1, f], beyond))
        for z in range(depth):
            last = z == depth - 1
            o = [opac[z, i] for i in range(2 if last else 3)]
            for f in range(BATCH):
                one, two, out = states[f]
                d1, d2, dh = (pltpu.roll(v, 1, 0) for v in (one, two, out))
                u1, u2, uh = (pltpu.roll(v, ROWS - 1, 0) for v in (one, two, out))
                winds = [
                    jnp.where(top_left, dh, jnp.where(low_right, u2, jnp.where(left, d1, u1))),
                    jnp.where(top_left, d1, jnp.where(low_right, uh, jnp.where(left, d2, u2))),
                    jnp.where(left, dh, uh),
                ]
                fresh = []
                for i in range(len(o)):
                    s = src[indices[f], z, i]
                    a = jnp.exp(rates[f] * o[i])
                    mixed = (1.0 - TILT_SHARE) * states[f][i] + TILT_SHARE * winds[i]
                    fresh.append(s + a * (mixed - s))
                if last:
                    fresh.append(out)
                states[f] = tuple(fresh)
            for half in range(2):
                for t in range(LINES):
                    total = acc[t, z, half]
                    for f in range(BATCH):
                        total = total + weights[f][t] * states[f][half]
                    acc[t, z, half] = total
        for f in range(BATCH):
            face_out[chunk, 0, f] = states[f][0]
            face_out[chunk, 1, f] = states[f][1]

        @pl.when(has_down)
        def _():
            main.start()

        @pl.when(has_down & has_right)
        def _():
            to_right.start()

        @pl.when(has_down & has_left)
        def _():
            to_left.start()

    def group_step(k, carry):
        for sub in range(subs):
            chunk_step(k, sub)
        return carry

    lax.fori_loop(0, bands, group_step, 0)

    beside = band + 1 - 2 * lax.rem(band, 2)
    across = lax.rem(band + 2, bands)
    corner = bands - 1 - band

    def gather_copy(kind, owner, zp, to):
        return pltpu.make_async_remote_copy(
            src_ref=gathered.at[owner, zp],
            dst_ref=gathered.at[owner, zp],
            send_sem=gat_send.at[kind, zp],
            recv_sem=gat_recv.at[kind, zp],
            device_id={"band": to},
            device_id_type=MESH,
        )

    def relax(zp, carry):
        for half in range(2):
            both = []
            for z in (zp, zp + pairs):
                p = COLLISION * plk[z, half]
                ratios = []
                for t in range(LINES):
                    j = acc[t, z, half]
                    j = j + half_turn(j)
                    ratios.append((j + p) / ((1.0 + COLLISION) + j))
                one = 0.5 * (ratios[0] / ratios[2] + ratios[1] / ratios[3])
                levels = (one, ratios[1] / ratios[4], ratios[0], ratios[1])
                both.append(levels)
                scale = 1.0 / (1.0 + levels[0] + levels[1] + levels[2] + levels[3])
                rows = pl.ds(half * ROWS, ROWS)
                pops_out[0, z, rows] = scale[:, :HALF]
                for i in range(4):
                    pops_out[1 + i, z, rows] = (scale * levels[i])[:, :HALF]
            for i in range(4):
                gathered[band, zp, i, half] = jnp.where(left, both[0][i], both[1][i])
        gather_copy(0, band, zp, beside).start()
        gather_copy(1, band, zp, across).start()
        return carry

    lax.fori_loop(0, pairs, relax, 0)

    loads[6].wait()

    def forward(q, carry):
        gather_copy(0, beside, 2 * q, beside).wait_recv()
        gather_copy(2, beside, 2 * q, across).start()
        gather_copy(1, across, 2 * q + 1, across).wait_recv()
        gather_copy(2, across, 2 * q + 1, beside).start()
        return carry

    lax.fori_loop(0, pairs // 2, forward, 0)

    def finish_two(q, carry):
        gather_copy(1, across, 2 * q, across).wait_recv()
        gather_copy(2, corner, 2 * q, corner).wait_recv()
        finish(2 * q)
        gather_copy(0, beside, 2 * q + 1, beside).wait_recv()
        gather_copy(2, corner, 2 * q + 1, corner).wait_recv()
        finish(2 * q + 1)
        return carry

    def finish(zp):
        for pair in range(bands // 2):
            columns = slice(pair * LANES, (pair + 1) * LANES)
            for half in range(2):
                rows = pl.ds(half * ROWS, ROWS)
                lines = []
                for b in (2 * pair, 2 * pair + 1):
                    levels = [1.0] + [gathered[b, zp, i, half] for i in range(4)]
                    lines.append(
                        [
                            levels[UPPER_LEVEL[t]] / (levels[LOWER_LEVEL[t]] + levels[UPPER_LEVEL[t]])
                            for t in range(LINES)
                        ]
                    )
                first = EPS_THERMAL * planck_all[zp, rows, columns]
                second = EPS_THERMAL * planck_all[zp + pairs, rows, columns]
                for t in range(LINES):
                    even, odd = lines[0][t], lines[1][t]
                    new_src[t, zp, rows, columns] = first + (1.0 - EPS_THERMAL) * jnp.where(
                        left, even, half_turn(odd)
                    )
                    new_src[t, zp + pairs, rows, columns] = second + (
                        1.0 - EPS_THERMAL
                    ) * jnp.where(left, half_turn(even), odd)
        for f in range(freqs):
            t = line_index[f]
            source_out[f, zp] = new_src[t, zp]
            source_out[f, zp + pairs] = new_src[t, zp + pairs]

    lax.fori_loop(0, pairs // 2, finish_two, 0)

    for k in range(1, bands):
        for copy in par_copies(k):
            copy.wait_send()

    @pl.when(has_right)
    def _():
        halo_copy(0).wait_send()

    @pl.when(has_left)
    def _():
        halo_copy(1).wait_send()

    def drain(chunk, carry):
        main, to_right, to_left = face_copies(chunk)

        @pl.when(has_down)
        def _():
            main.wait_send()

        @pl.when(has_down & has_right)
        def _():
            to_right.wait_send()

        @pl.when(has_down & has_left)
        def _():
            to_left.wait_send()

        return carry

    lax.fori_loop(0, bands * subs, drain, 0)

    def drain_gather(zp, carry):
        gather_copy(0, band, zp, beside).wait_send()
        gather_copy(1, band, zp, across).wait_send()
        gather_copy(2, corner, zp, across).wait_send()
        return carry

    lax.fori_loop(0, pairs, drain_gather, 0)


def write_out(pops, source, pops_hbm, source_hbm, sem):
    copies = [pltpu.make_async_copy(pops, pops_hbm, sem.at[0])]
    for f in range(source.shape[0]):
        copies.append(pltpu.make_async_copy(source.at[f], source_hbm.at[f], sem.at[1 + f]))
    for copy in copies:
        copy.start()
    for copy in copies:
        copy.wait()


def per_device(sizes, strength, opacity, planck, old_populations, line_index, line_weight):
    bands, tiles, slabs = sizes
    depth, rows, cells = opacity.shape
    freqs = strength.shape[0]
    pairs = depth // 2
    chunks = bands * freqs // BATCH
    assert rows == 2 * ROWS and depth == ROWS and cells == bands * HALF and bands == 4
    f32 = jnp.float32
    hbm = pl.BlockSpec(memory_space=pltpu.HBM)
    vmem = pl.BlockSpec(memory_space=pltpu.VMEM)
    sem = pltpu.SemaphoreType.DMA
    tile = (ROWS, LANES)
    pops, source = pl.pallas_call(
        functools.partial(kernel, (bands, tiles, slabs, depth, freqs)),
        out_shape=(
            jax.ShapeDtypeStruct((LEVELS, depth, rows, cells // bands), f32),
            jax.ShapeDtypeStruct((freqs, depth, rows, cells), f32),
        ),
        in_specs=[hbm] * 6,
        out_specs=(vmem, vmem),
        scratch_shapes=[
            pltpu.SMEM((freqs,), f32),
            pltpu.SMEM((freqs,), jnp.int32),
            pltpu.SMEM((freqs,), f32),
            pltpu.VMEM((2 + LEVELS, depth, rows, LANES), f32),
            pltpu.VMEM((depth, rows, cells), f32),
            pltpu.VMEM((bands, 3) + tile, f32),
            pltpu.VMEM((bands, 1, LANES), jnp.int32),
            pltpu.SMEM((bands, 1, LANES), jnp.int32),
            pltpu.VMEM((2, 1 + LINES, pairs // 2) + tile, f32),
            pltpu.VMEM((2, 1 + LINES, pairs // 2) + tile, f32),
            pltpu.VMEM((depth, 3) + tile, f32),
            pltpu.VMEM((LINES, depth, 3) + tile, f32),
            pltpu.VMEM((depth, 2) + tile, f32),
            pltpu.VMEM((chunks, 2, BATCH) + tile, f32),
            pltpu.VMEM((2, chunks, BATCH) + tile, f32),
            pltpu.VMEM((chunks, 2, BATCH) + tile, f32),
            pltpu.VMEM((LINES, depth, 2) + tile, f32),
            pltpu.VMEM((bands, pairs, 4, 2) + tile, f32),
            pltpu.VMEM((LINES, depth, rows, cells), f32),
            sem((7,)),
            sem,
            sem((2, bands)),
            sem((2, bands)),
            sem((2,)),
            sem((2,)),
            sem((3, chunks)),
            sem((3, chunks)),
            sem((3, pairs)),
            sem((3, pairs)),
        ],
        compiler_params=pltpu.CompilerParams(
            collective_id=0, has_side_effects=True, vmem_limit_bytes=32 * 1024 * 1024
        ),
        cost_estimate=pl.CostEstimate(
            flops=60 * depth * rows * cells * freqs,
            bytes_accessed=16 * depth * rows * cells * 4,
            transcendentals=2 * depth * rows * cells * freqs,
        ),
    )(
        *(
            pltpu.with_memory_space_constraint(v, pltpu.HBM)
            for v in (strength, line_index, line_weight, opacity, planck, old_populations)
        )
    )
    return pl.pallas_call(
        write_out,
        out_shape=(
            jax.ShapeDtypeStruct(pops.shape, f32),
            jax.ShapeDtypeStruct(source.shape, f32),
        ),
        in_specs=[vmem] * 2,
        out_specs=(hbm, hbm),
        scratch_shapes=[sem((1 + freqs,))],
    )(
        pltpu.with_memory_space_constraint(pops, pltpu.VMEM),
        pltpu.with_memory_space_constraint(source, pltpu.VMEM),
    )


def solution(mesh):
    sizes = (mesh.shape["band"], mesh.shape["tile"], mesh.shape["slab"])
    in_specs = (
        P("band"),
        P("slab", "tile", None),
        P("slab", "tile", None),
        P(None, "slab", "tile", None),
        P("band"),
        P("band"),
    )
    out_specs = (P(None, "slab", "tile", "band"), P("band", "slab", "tile", None))
    return jax.shard_map(
        functools.partial(per_device, sizes),
        mesh=mesh,
        in_specs=in_specs,
        out_specs=out_specs,
        check_vma=False,
    )
```

```python
import functools

import jax
import jax.numpy as jnp
from jax import lax
from jax.experimental import pallas as pl
from jax.experimental.pallas import tpu as pltpu
from jax.sharding import PartitionSpec as P

MESH = pl.DeviceIdType.MESH
LINES = 5
LEVELS = 5
EPS_THERMAL = 0.1
COLLISION = 0.5
PATH_FACTOR = 1.25
TILT_SHARE = 0.4
LOWER_LEVEL = (0, 0, 1, 1, 2)
UPPER_LEVEL = (3, 4, 3, 4, 4)
LANES = 128
ROWS = 8
HALF = LANES // 2
BATCH = 4


def half_turn(v):
    return pltpu.roll(v, HALF, 1)


def kernel(
    sizes,
    strength_hbm,
    line_index_hbm,
    line_weight_hbm,
    opacity,
    planck,
    populations,
    pops_out,
    source_out,
    strength,
    line_index,
    line_weight,
    fields,
    planck_all,
    par_f,
    par_i,
    par_s,
    halo_out,
    halo_in,
    opac,
    src,
    plk,
    face_in,
    face_halo,
    face_out,
    acc,
    gathered,
    new_src,
    in_sem,
    idx_sem,
    par_send,
    par_recv,
    halo_send,
    halo_recv,
    face_send,
    face_recv,
    gat_send,
    gat_recv,
):
    bands, tiles, slabs, depth, freqs = sizes
    pairs = depth // 2
    subs = freqs // BATCH
    band = lax.axis_index("band")
    tile = lax.axis_index("tile")
    slab = lax.axis_index("slab")
    has_left = tile > 0
    has_right = tile < tiles - 1
    has_up = slab > 0
    has_down = slab < slabs - 1

    column = pl.multiple_of((band // 2) * LANES, LANES)
    loads = [
        pltpu.make_async_copy(opacity.at[:, :, pl.ds(column, LANES)], fields.at[0], in_sem.at[0]),
        pltpu.make_async_copy(planck.at[:, :, pl.ds(column, LANES)], fields.at[1], in_sem.at[1]),
        pltpu.make_async_copy(
            populations.at[:, :, :, pl.ds(column, LANES)], fields.at[pl.ds(2, LEVELS)], in_sem.at[2]
        ),
        pltpu.make_async_copy(strength_hbm, strength, in_sem.at[3]),
        pltpu.make_async_copy(line_index_hbm, line_index, in_sem.at[4]),
        pltpu.make_async_copy(line_weight_hbm, line_weight, in_sem.at[5]),
        pltpu.make_async_copy(planck, planck_all, in_sem.at[6]),
    ]
    for load in loads:
        load.start()

    barrier = pltpu.get_barrier_semaphore()
    for k in range(1, bands):
        pl.semaphore_signal(
            barrier, inc=1, device_id={"band": lax.rem(band + k, bands)}, device_id_type=MESH
        )
    expected = jnp.int32(bands - 1)
    for dt in (-1, 0, 1):
        for ds in (-1, 0, 1):
            if dt == 0 and ds == 0:
                continue
            there = (tile + dt >= 0) & (tile + dt < tiles) & (slab + ds >= 0) & (slab + ds < slabs)

            @pl.when(there)
            def _():
                pl.semaphore_signal(
                    barrier,
                    inc=1,
                    device_id={"tile": tile + dt, "slab": slab + ds},
                    device_id_type=MESH,
                )

            expected = expected + there.astype(jnp.int32)

    row = lax.broadcasted_iota(jnp.int32, (ROWS, LANES), 0)
    lane = lax.broadcasted_iota(jnp.int32, (ROWS, LANES), 1)
    left = lane < HALF
    own = (lane // HALF) == lax.rem(band, 2)
    top_left = left & (row == 0)
    low_right = jnp.logical_not(left) & (row == ROWS - 1)

    @pl.when(jnp.logical_not(has_left))
    def _():
        halo_in[0] = jnp.zeros(halo_in.shape[1:], jnp.float32)
        face_halo[0] = jnp.zeros(face_halo.shape[1:], jnp.float32)

    @pl.when(jnp.logical_not(has_right))
    def _():
        halo_in[1] = jnp.zeros(halo_in.shape[1:], jnp.float32)
        face_halo[1] = jnp.zeros(face_halo.shape[1:], jnp.float32)

    @pl.when(jnp.logical_not(has_up))
    def _():
        face_in[...] = jnp.zeros(face_in.shape, jnp.float32)
        face_halo[...] = jnp.zeros(face_halo.shape, jnp.float32)

    acc[0] = jnp.zeros(acc.shape[1:], jnp.float32)

    def par_copies(k):
        to = {"band": lax.rem(band + k, bands)}
        return (
            pltpu.make_async_remote_copy(
                src_ref=par_f.at[0],
                dst_ref=par_f.at[k],
                send_sem=par_send.at[0, k],
                recv_sem=par_recv.at[0, k],
                device_id=to,
                device_id_type=MESH,
            ),
            pltpu.make_async_remote_copy(
                src_ref=par_i.at[0],
                dst_ref=par_i.at[k],
                send_sem=par_send.at[1, k],
                recv_sem=par_recv.at[1, k],
                device_id=to,
                device_id_type=MESH,
            ),
        )

    for load in loads[:6]:
        load.wait()

    lane_row = lax.broadcasted_iota(jnp.int32, (1, LANES), 1)
    indices = jnp.zeros((1, LANES), jnp.int32)
    zero = jnp.zeros((ROWS, LANES), jnp.float32)
    rate, weight = zero, zero
    for f in range(freqs):
        here = row == f
        rate = jnp.where(here, -PATH_FACTOR * strength[f], rate)
        weight = jnp.where(here, line_weight[f] * (LINES / (2.0 * freqs * bands)), weight)
        indices = jnp.where(lane_row == f, line_index[f], indices)
    par_f[0, 0] = rate
    par_f[0, 1] = weight
    par_i[0] = indices

    def spread(v):
        return jnp.where(own, v, half_turn(v))

    def prepare(z, carry):
        for half in range(2):
            rows = pl.ds(half * ROWS, ROWS)
            p = spread(fields[1, z, rows])
            levels = [spread(fields[2 + i, z, rows]) for i in range(LEVELS)]
            opac[z, half] = spread(fields[0, z, rows])
            plk[z, half] = p
            for t in range(LINES):
                low, up = levels[LOWER_LEVEL[t]], levels[UPPER_LEVEL[t]]
                src[t, z, half] = EPS_THERMAL * p + (1.0 - EPS_THERMAL) * (up / (low + up))
        return carry

    for z in range(depth):
        prepare(z, 0)

    def layer(i, z, part):
        return opac[z, part] if i == 0 else src[i - 1, z, part]

    for i in range(1 + LINES):
        right, down = [], []
        for z in range(pairs):
            y = depth - 2 - z
            a, b = layer(i, z, 1), layer(i, z, 0)
            if y > z:
                a = jnp.where(row >= 1 + z, a, pltpu.roll(layer(i, y, 1), z + 1, 0))
                b = jnp.where(row <= y, b, pltpu.roll(layer(i, y, 0), y + 1, 0))
            right.append(a)
            down.append(b)
        for q in range(pairs // 2):
            halo_out[0, i, q] = jnp.where(left, right[q], right[q + pairs // 2])
            halo_out[1, i, q] = jnp.where(left, down[q + pairs // 2], down[q])

    pl.semaphore_wait(barrier, expected)
    for k in range(1, bands):
        for copy in par_copies(k):
            copy.start()

    def halo_copy(side):
        return pltpu.make_async_remote_copy(
            src_ref=halo_out.at[side],
            dst_ref=halo_in.at[side],
            send_sem=halo_send.at[side],
            recv_sem=halo_recv.at[side],
            device_id={"tile": tile + (1 if side == 0 else -1)},
            device_id_type=MESH,
        )

    @pl.when(has_right)
    def _():
        halo_copy(0).start()

    @pl.when(has_left)
    def _():
        halo_copy(1).start()

    for k in range(1, bands):
        for copy in par_copies(k):
            copy.wait_recv()
    to_scalars = pltpu.make_async_copy(par_i, par_s, idx_sem)
    to_scalars.start()
    to_scalars.wait()

    @pl.when(has_left)
    def _():
        halo_copy(0).wait_recv()

    @pl.when(has_right)
    def _():
        halo_copy(1).wait_recv()

    for i in range(1 + LINES):
        for q in range(pairs // 2):
            a, b = halo_in[0, i, q], halo_in[1, i, q]
            shared = {q: jnp.where(left, a, b)}
            shared[q + pairs // 2] = half_turn(jnp.where(left, b, a))
            for z, tile_rows in shared.items():
                y = depth - 2 - z
                both = [(z, tile_rows)]
                if y > z:
                    moved = (pltpu.roll(tile_rows, y + 1, 0), pltpu.roll(tile_rows, z + 1, 0))
                    both.append((y, jnp.where(left, *moved)))
                for at, v in both:
                    if i == 0:
                        opac[at, 2] = v
                    else:
                        src[i - 1, at, 2] = v

    def face_copies(chunk):
        def make(part, source, target, to):
            return pltpu.make_async_remote_copy(
                src_ref=source,
                dst_ref=target,
                send_sem=face_send.at[part, chunk],
                recv_sem=face_recv.at[part, chunk],
                device_id=to,
                device_id_type=MESH,
            )

        return (
            make(0, face_out.at[chunk], face_in.at[chunk], {"slab": slab + 1}),
            make(
                1,
                face_out.at[chunk, 1],
                face_halo.at[0, chunk],
                {"tile": tile + 1, "slab": slab + 1},
            ),
            make(
                2,
                face_out.at[chunk, 0],
                face_halo.at[1, chunk],
                {"tile": tile - 1, "slab": slab + 1},
            ),
        )

    def chunk_step(k, sub, latest):
        chunk = k * subs + sub
        main, to_right, to_left = face_copies(chunk)

        @pl.when(has_up)
        def _():
            main.wait_recv()

        @pl.when(has_up & has_left)
        def _():
            to_right.wait_recv()

        @pl.when(has_up & has_right)
        def _():
            to_left.wait_recv()

        states, rates, weights, indices, before, slots = [], [], [], [], [], []
        for f in range(BATCH):
            at = pl.ds(sub * BATCH + f, 1)
            rates.append(jnp.broadcast_to(par_f[k, 0, at], (ROWS, LANES)))
            weights.append(jnp.broadcast_to(par_f[k, 1, at], (ROWS, LANES)))
            line = par_s[k, 0, sub * BATCH + f]
            indices.append(line)
            slot = k * freqs + (sub * BATCH + f + 1)
            previous = latest[0]
            for t in range(1, LINES):
                previous = jnp.where(line == t, latest[t], previous)
            latest = [jnp.where(line == t, slot, latest[t]) for t in range(LINES)]
            before.append(previous)
            slots.append(slot)
            beyond = jnp.where(left, face_halo[0, chunk, f], face_halo[1, chunk, f])
            states.append((face_in[chunk, 0, f], face_in[chunk, 1, f], beyond))
        for z in range(depth):
            last = z == depth - 1
            o = [opac[z, i] for i in range(2 if last else 3)]
            for f in range(BATCH):
                one, two, out = states[f]
                d1, d2, dh = (pltpu.roll(v, 1, 0) for v in (one, two, out))
                u1, u2, uh = (pltpu.roll(v, ROWS - 1, 0) for v in (one, two, out))
                winds = [
                    jnp.where(top_left, dh, jnp.where(low_right, u2, jnp.where(left, d1, u1))),
                    jnp.where(top_left, d1, jnp.where(low_right, uh, jnp.where(left, d2, u2))),
                    jnp.where(left, dh, uh),
                ]
                fresh = []
                for i in range(len(o)):
                    s = src[indices[f], z, i]
                    a = jnp.exp(rates[f] * o[i])
                    mixed = (1.0 - TILT_SHARE) * states[f][i] + TILT_SHARE * winds[i]
                    fresh.append(s + a * (mixed - s))
                if last:
                    fresh.append(out)
                states[f] = tuple(fresh)
            for half in range(2):
                for f in range(BATCH):
                    acc[slots[f], z, half] = acc[before[f], z, half] + weights[f] * states[f][half]
        for f in range(BATCH):
            face_out[chunk, 0, f] = states[f][0]
            face_out[chunk, 1, f] = states[f][1]

        @pl.when(has_down)
        def _():
            main.start()

        @pl.when(has_down & has_right)
        def _():
            to_right.start()

        @pl.when(has_down & has_left)
        def _():
            to_left.start()

        return latest

    def group_step(k, latest):
        for sub in range(subs):
            latest = chunk_step(k, sub, latest)
        return tuple(latest)

    latest = lax.fori_loop(0, bands, group_step, (jnp.int32(0),) * LINES)

    beside = band + 1 - 2 * lax.rem(band, 2)
    across = lax.rem(band + 2, bands)
    corner = bands - 1 - band

    def gather_copy(kind, owner, zp, to):
        return pltpu.make_async_remote_copy(
            src_ref=gathered.at[owner, zp],
            dst_ref=gathered.at[owner, zp],
            send_sem=gat_send.at[kind, zp],
            recv_sem=gat_recv.at[kind, zp],
            device_id={"band": to},
            device_id_type=MESH,
        )

    def relax(zp, carry):
        for half in range(2):
            both = []
            for z in (zp, zp + pairs):
                p = COLLISION * plk[z, half]
                ratios = []
                for t in range(LINES):
                    j = acc[latest[t], z, half]
                    j = j + half_turn(j)
                    ratios.append((j + p) / ((1.0 + COLLISION) + j))
                one = 0.5 * (ratios[0] / ratios[2] + ratios[1] / ratios[3])
                levels = (one, ratios[1] / ratios[4], ratios[0], ratios[1])
                both.append(levels)
                scale = 1.0 / (1.0 + levels[0] + levels[1] + levels[2] + levels[3])
                rows = pl.ds(half * ROWS, ROWS)
                pops_out[0, z, rows] = scale[:, :HALF]
                for i in range(4):
                    pops_out[1 + i, z, rows] = (scale * levels[i])[:, :HALF]
            for i in range(4):
                gathered[band, zp, i, half] = jnp.where(left, both[0][i], both[1][i])
        gather_copy(0, band, zp, beside).start()
        gather_copy(1, band, zp, across).start()
        return carry

    for zp in range(pairs):
        relax(zp, 0)

    loads[6].wait()

    def forward(q, carry):
        gather_copy(0, beside, 2 * q, beside).wait_recv()
        gather_copy(2, beside, 2 * q, across).start()
        gather_copy(1, across, 2 * q + 1, across).wait_recv()
        gather_copy(2, across, 2 * q + 1, beside).start()
        return carry

    lax.fori_loop(0, pairs // 2, forward, 0)

    def finish_two(q, carry):
        gather_copy(1, across, 2 * q, across).wait_recv()
        gather_copy(2, corner, 2 * q, corner).wait_recv()
        finish(2 * q)
        gather_copy(0, beside, 2 * q + 1, beside).wait_recv()
        gather_copy(2, corner, 2 * q + 1, corner).wait_recv()
        finish(2 * q + 1)
        return carry

    def finish(zp):
        for pair in range(bands // 2):
            columns = slice(pair * LANES, (pair + 1) * LANES)
            for half in range(2):
                rows = pl.ds(half * ROWS, ROWS)
                lines = []
                for b in (2 * pair, 2 * pair + 1):
                    levels = [1.0] + [gathered[b, zp, i, half] for i in range(4)]
                    lines.append(
                        [
                            levels[UPPER_LEVEL[t]] / (levels[LOWER_LEVEL[t]] + levels[UPPER_LEVEL[t]])
                            for t in range(LINES)
                        ]
                    )
                first = EPS_THERMAL * planck_all[zp, rows, columns]
                second = EPS_THERMAL * planck_all[zp + pairs, rows, columns]
                for t in range(LINES):
                    even, odd = lines[0][t], lines[1][t]
                    new_src[t, zp, rows, columns] = first + (1.0 - EPS_THERMAL) * jnp.where(
                        left, even, half_turn(odd)
                    )
                    new_src[t, zp + pairs, rows, columns] = second + (
                        1.0 - EPS_THERMAL
                    ) * jnp.where(left, half_turn(even), odd)
        for f in range(freqs):
            t = line_index[f]
            source_out[f, zp] = new_src[t, zp]
            source_out[f, zp + pairs] = new_src[t, zp + pairs]

    lax.fori_loop(0, pairs // 2, finish_two, 0)

    for k in range(1, bands):
        for copy in par_copies(k):
            copy.wait_send()

    @pl.when(has_right)
    def _():
        halo_copy(0).wait_send()

    @pl.when(has_left)
    def _():
        halo_copy(1).wait_send()

    def drain(chunk, carry):
        main, to_right, to_left = face_copies(chunk)

        @pl.when(has_down)
        def _():
            main.wait_send()

        @pl.when(has_down & has_right)
        def _():
            to_right.wait_send()

        @pl.when(has_down & has_left)
        def _():
            to_left.wait_send()

        return carry

    lax.fori_loop(0, bands * subs, drain, 0)

    def drain_gather(zp, carry):
        gather_copy(0, band, zp, beside).wait_send()
        gather_copy(1, band, zp, across).wait_send()
        gather_copy(2, corner, zp, across).wait_send()
        return carry

    lax.fori_loop(0, pairs, drain_gather, 0)


def write_out(pops, source, pops_hbm, source_hbm, sem):
    copies = [pltpu.make_async_copy(pops, pops_hbm, sem.at[0])]
    for f in range(source.shape[0]):
        copies.append(pltpu.make_async_copy(source.at[f], source_hbm.at[f], sem.at[1 + f]))
    for copy in copies:
        copy.start()
    for copy in copies:
        copy.wait()


def per_device(sizes, strength, opacity, planck, old_populations, line_index, line_weight):
    bands, tiles, slabs = sizes
    depth, rows, cells = opacity.shape
    freqs = strength.shape[0]
    pairs = depth // 2
    chunks = bands * freqs // BATCH
    assert rows == 2 * ROWS and depth == ROWS and cells == bands * HALF and bands == 4
    f32 = jnp.float32
    hbm = pl.BlockSpec(memory_space=pltpu.HBM)
    vmem = pl.BlockSpec(memory_space=pltpu.VMEM)
    sem = pltpu.SemaphoreType.DMA
    tile = (ROWS, LANES)
    pops, source = pl.pallas_call(
        functools.partial(kernel, (bands, tiles, slabs, depth, freqs)),
        out_shape=(
            jax.ShapeDtypeStruct((LEVELS, depth, rows, cells // bands), f32),
            jax.ShapeDtypeStruct((freqs, depth, rows, cells), f32),
        ),
        in_specs=[hbm] * 6,
        out_specs=(vmem, vmem),
        scratch_shapes=[
            pltpu.SMEM((freqs,), f32),
            pltpu.SMEM((freqs,), jnp.int32),
            pltpu.SMEM((freqs,), f32),
            pltpu.VMEM((2 + LEVELS, depth, rows, LANES), f32),
            pltpu.VMEM((depth, rows, cells), f32),
            pltpu.VMEM((bands, 2) + tile, f32),
            pltpu.VMEM((bands, 1, LANES), jnp.int32),
            pltpu.SMEM((bands, 1, LANES), jnp.int32),
            pltpu.VMEM((2, 1 + LINES, pairs // 2) + tile, f32),
            pltpu.VMEM((2, 1 + LINES, pairs // 2) + tile, f32),
            pltpu.VMEM((depth, 3) + tile, f32),
            pltpu.VMEM((LINES, depth, 3) + tile, f32),
            pltpu.VMEM((depth, 2) + tile, f32),
            pltpu.VMEM((chunks, 2, BATCH) + tile, f32),
            pltpu.VMEM((2, chunks, BATCH) + tile, f32),
            pltpu.VMEM((chunks, 2, BATCH) + tile, f32),
            pltpu.VMEM((1 + bands * freqs, depth, 2) + tile, f32),
            pltpu.VMEM((bands, pairs, 4, 2) + tile, f32),
            pltpu.VMEM((LINES, depth, rows, cells), f32),
            sem((7,)),
            sem,
            sem((2, bands)),
            sem((2, bands)),
            sem((2,)),
            sem((2,)),
            sem((3, chunks)),
            sem((3, chunks)),
            sem((3, pairs)),
            sem((3, pairs)),
        ],
        compiler_params=pltpu.CompilerParams(
            collective_id=0, has_side_effects=True, vmem_limit_bytes=32 * 1024 * 1024
        ),
        cost_estimate=pl.CostEstimate(
            flops=60 * depth * rows * cells * freqs,
            bytes_accessed=16 * depth * rows * cells * 4,
            transcendentals=2 * depth * rows * cells * freqs,
        ),
    )(
        *(
            pltpu.with_memory_space_constraint(v, pltpu.HBM)
            for v in (strength, line_index, line_weight, opacity, planck, old_populations)
        )
    )
    return pl.pallas_call(
        write_out,
        out_shape=(
            jax.ShapeDtypeStruct(pops.shape, f32),
            jax.ShapeDtypeStruct(source.shape, f32),
        ),
        in_specs=[vmem] * 2,
        out_specs=(hbm, hbm),
        scratch_shapes=[sem((1 + freqs,))],
    )(
        pltpu.with_memory_space_constraint(pops, pltpu.VMEM),
        pltpu.with_memory_space_constraint(source, pltpu.VMEM),
    )


def solution(mesh):
    sizes = (mesh.shape["band"], mesh.shape["tile"], mesh.shape["slab"])
    in_specs = (
        P("band"),
        P("slab", "tile", None),
        P("slab", "tile", None),
        P(None, "slab", "tile", None),
        P("band"),
        P("band"),
    )
    out_specs = (P(None, "slab", "tile", "band"), P("band", "slab", "tile", None))
    return jax.shard_map(
        functools.partial(per_device, sizes),
        mesh=mesh,
        in_specs=in_specs,
        out_specs=out_specs,
        check_vma=False,
    )
```

```python
import functools

import jax
import jax.numpy as jnp
from jax import lax
from jax.experimental import pallas as pl
from jax.experimental.pallas import tpu as pltpu
from jax.sharding import PartitionSpec as P

MESH = pl.DeviceIdType.MESH
LINES = 5
LEVELS = 5
EPS_THERMAL = 0.1
COLLISION = 0.5
PATH_FACTOR = 1.25
TILT_SHARE = 0.4
LOWER_LEVEL = (0, 0, 1, 1, 2)
UPPER_LEVEL = (3, 4, 3, 4, 4)
LANES = 128
ROWS = 8
HALF = LANES // 2
BATCH = 8


def half_turn(v):
    return pltpu.roll(v, HALF, 1)


def kernel(
    sizes,
    strength_hbm,
    line_index_hbm,
    line_weight_hbm,
    opacity,
    planck,
    populations,
    pops_out,
    source_out,
    strength,
    line_index,
    line_weight,
    fields,
    planck_all,
    par_f,
    par_i,
    par_s,
    halo_out,
    halo_in,
    opac,
    src,
    plk,
    face_in,
    face_halo,
    face_out,
    acc,
    gathered,
    new_src,
    in_sem,
    idx_sem,
    par_send,
    par_recv,
    halo_send,
    halo_recv,
    face_send,
    face_recv,
    gat_send,
    gat_recv,
):
    bands, tiles, slabs, depth, freqs = sizes
    pairs = depth // 2
    subs = freqs // BATCH
    band = lax.axis_index("band")
    tile = lax.axis_index("tile")
    slab = lax.axis_index("slab")
    has_left = tile > 0
    has_right = tile < tiles - 1
    has_up = slab > 0
    has_down = slab < slabs - 1

    column = pl.multiple_of((band // 2) * LANES, LANES)
    loads = [
        pltpu.make_async_copy(opacity.at[:, :, pl.ds(column, LANES)], fields.at[0], in_sem.at[0]),
        pltpu.make_async_copy(planck.at[:, :, pl.ds(column, LANES)], fields.at[1], in_sem.at[1]),
        pltpu.make_async_copy(
            populations.at[:, :, :, pl.ds(column, LANES)], fields.at[pl.ds(2, LEVELS)], in_sem.at[2]
        ),
        pltpu.make_async_copy(strength_hbm, strength, in_sem.at[3]),
        pltpu.make_async_copy(line_index_hbm, line_index, in_sem.at[4]),
        pltpu.make_async_copy(line_weight_hbm, line_weight, in_sem.at[5]),
        pltpu.make_async_copy(planck, planck_all, in_sem.at[6]),
    ]
    for load in loads:
        load.start()

    barrier = pltpu.get_barrier_semaphore()
    for k in range(1, bands):
        pl.semaphore_signal(
            barrier, inc=1, device_id={"band": lax.rem(band + k, bands)}, device_id_type=MESH
        )
    expected = jnp.int32(bands - 1)
    for dt in (-1, 0, 1):
        for ds in (-1, 0, 1):
            if dt == 0 and ds == 0:
                continue
            there = (tile + dt >= 0) & (tile + dt < tiles) & (slab + ds >= 0) & (slab + ds < slabs)

            @pl.when(there)
            def _():
                pl.semaphore_signal(
                    barrier,
                    inc=1,
                    device_id={"tile": tile + dt, "slab": slab + ds},
                    device_id_type=MESH,
                )

            expected = expected + there.astype(jnp.int32)

    row = lax.broadcasted_iota(jnp.int32, (ROWS, LANES), 0)
    lane = lax.broadcasted_iota(jnp.int32, (ROWS, LANES), 1)
    left = lane < HALF
    own = (lane // HALF) == lax.rem(band, 2)
    top_left = left & (row == 0)
    low_right = jnp.logical_not(left) & (row == ROWS - 1)

    @pl.when(jnp.logical_not(has_left))
    def _():
        halo_in[0] = jnp.zeros(halo_in.shape[1:], jnp.float32)
        face_halo[0] = jnp.zeros(face_halo.shape[1:], jnp.float32)

    @pl.when(jnp.logical_not(has_right))
    def _():
        halo_in[1] = jnp.zeros(halo_in.shape[1:], jnp.float32)
        face_halo[1] = jnp.zeros(face_halo.shape[1:], jnp.float32)

    @pl.when(jnp.logical_not(has_up))
    def _():
        face_in[...] = jnp.zeros(face_in.shape, jnp.float32)
        face_halo[...] = jnp.zeros(face_halo.shape, jnp.float32)

    acc[0] = jnp.zeros(acc.shape[1:], jnp.float32)

    def par_copies(k):
        to = {"band": lax.rem(band + k, bands)}
        return (
            pltpu.make_async_remote_copy(
                src_ref=par_f.at[0],
                dst_ref=par_f.at[k],
                send_sem=par_send.at[0, k],
                recv_sem=par_recv.at[0, k],
                device_id=to,
                device_id_type=MESH,
            ),
            pltpu.make_async_remote_copy(
                src_ref=par_i.at[0],
                dst_ref=par_i.at[k],
                send_sem=par_send.at[1, k],
                recv_sem=par_recv.at[1, k],
                device_id=to,
                device_id_type=MESH,
            ),
        )

    for load in loads[:6]:
        load.wait()

    lane_row = lax.broadcasted_iota(jnp.int32, (1, LANES), 1)
    indices = jnp.zeros((1, LANES), jnp.int32)
    zero = jnp.zeros((ROWS, LANES), jnp.float32)
    rate, weight = zero, zero
    for f in range(freqs):
        here = row == f
        rate = jnp.where(here, -PATH_FACTOR * strength[f], rate)
        weight = jnp.where(here, line_weight[f] * (LINES / (2.0 * freqs * bands)), weight)
        indices = jnp.where(lane_row == f, line_index[f], indices)
    par_f[0, 0] = rate
    par_f[0, 1] = weight
    par_i[0] = indices

    def spread(v):
        return jnp.where(own, v, half_turn(v))

    def prepare(z, carry):
        for half in range(2):
            rows = pl.ds(half * ROWS, ROWS)
            p = spread(fields[1, z, rows])
            levels = [spread(fields[2 + i, z, rows]) for i in range(LEVELS)]
            opac[z, half] = spread(fields[0, z, rows])
            plk[z, half] = p
            for t in range(LINES):
                low, up = levels[LOWER_LEVEL[t]], levels[UPPER_LEVEL[t]]
                src[t, z, half] = EPS_THERMAL * p + (1.0 - EPS_THERMAL) * (up / (low + up))
        return carry

    for z in range(depth):
        prepare(z, 0)

    def layer(i, z, part):
        return opac[z, part] if i == 0 else src[i - 1, z, part]

    for i in range(1 + LINES):
        right, down = [], []
        for z in range(pairs):
            y = depth - 2 - z
            a, b = layer(i, z, 1), layer(i, z, 0)
            if y > z:
                a = jnp.where(row >= 1 + z, a, pltpu.roll(layer(i, y, 1), z + 1, 0))
                b = jnp.where(row <= y, b, pltpu.roll(layer(i, y, 0), y + 1, 0))
            right.append(a)
            down.append(b)
        for q in range(pairs // 2):
            halo_out[0, i, q] = jnp.where(left, right[q], right[q + pairs // 2])
            halo_out[1, i, q] = jnp.where(left, down[q + pairs // 2], down[q])

    pl.semaphore_wait(barrier, expected)
    for k in range(1, bands):
        for copy in par_copies(k):
            copy.start()

    def halo_copy(side):
        return pltpu.make_async_remote_copy(
            src_ref=halo_out.at[side],
            dst_ref=halo_in.at[side],
            send_sem=halo_send.at[side],
            recv_sem=halo_recv.at[side],
            device_id={"tile": tile + (1 if side == 0 else -1)},
            device_id_type=MESH,
        )

    @pl.when(has_right)
    def _():
        halo_copy(0).start()

    @pl.when(has_left)
    def _():
        halo_copy(1).start()

    for k in range(1, bands):
        for copy in par_copies(k):
            copy.wait_recv()
    to_scalars = pltpu.make_async_copy(par_i, par_s, idx_sem)
    to_scalars.start()
    to_scalars.wait()

    @pl.when(has_left)
    def _():
        halo_copy(0).wait_recv()

    @pl.when(has_right)
    def _():
        halo_copy(1).wait_recv()

    for i in range(1 + LINES):
        for q in range(pairs // 2):
            a, b = halo_in[0, i, q], halo_in[1, i, q]
            shared = {q: jnp.where(left, a, b)}
            shared[q + pairs // 2] = half_turn(jnp.where(left, b, a))
            for z, tile_rows in shared.items():
                y = depth - 2 - z
                both = [(z, tile_rows)]
                if y > z:
                    moved = (pltpu.roll(tile_rows, y + 1, 0), pltpu.roll(tile_rows, z + 1, 0))
                    both.append((y, jnp.where(left, *moved)))
                for at, v in both:
                    if i == 0:
                        opac[at, 2] = v
                    else:
                        src[i - 1, at, 2] = v

    def face_copies(chunk):
        def make(part, source, target, to):
            return pltpu.make_async_remote_copy(
                src_ref=source,
                dst_ref=target,
                send_sem=face_send.at[part, chunk],
                recv_sem=face_recv.at[part, chunk],
                device_id=to,
                device_id_type=MESH,
            )

        return (
            make(0, face_out.at[chunk], face_in.at[chunk], {"slab": slab + 1}),
            make(
                1,
                face_out.at[chunk, 1],
                face_halo.at[0, chunk],
                {"tile": tile + 1, "slab": slab + 1},
            ),
            make(
                2,
                face_out.at[chunk, 0],
                face_halo.at[1, chunk],
                {"tile": tile - 1, "slab": slab + 1},
            ),
        )

    def chunk_step(k, sub, latest):
        chunk = k * subs + sub
        main, to_right, to_left = face_copies(chunk)

        @pl.when(has_up)
        def _():
            main.wait_recv()

        @pl.when(has_up & has_left)
        def _():
            to_right.wait_recv()

        @pl.when(has_up & has_right)
        def _():
            to_left.wait_recv()

        states, rates, weights, indices, before, slots = [], [], [], [], [], []
        for f in range(BATCH):
            at = pl.ds(sub * BATCH + f, 1)
            rates.append(jnp.broadcast_to(par_f[k, 0, at], (ROWS, LANES)))
            weights.append(jnp.broadcast_to(par_f[k, 1, at], (ROWS, LANES)))
            line = par_s[k, 0, sub * BATCH + f]
            indices.append(line)
            slot = k * freqs + (sub * BATCH + f + 1)
            previous = latest[0]
            for t in range(1, LINES):
                previous = jnp.where(line == t, latest[t], previous)
            latest = [jnp.where(line == t, slot, latest[t]) for t in range(LINES)]
            before.append(previous)
            slots.append(slot)
            beyond = jnp.where(left, face_halo[0, chunk, f], face_halo[1, chunk, f])
            states.append((face_in[chunk, 0, f], face_in[chunk, 1, f], beyond))
        for z in range(depth):
            last = z == depth - 1
            o = [opac[z, i] for i in range(2 if last else 3)]
            for f in range(BATCH):
                one, two, out = states[f]
                d1, d2, dh = (pltpu.roll(v, 1, 0) for v in (one, two, out))
                u1, u2, uh = (pltpu.roll(v, ROWS - 1, 0) for v in (one, two, out))
                winds = [
                    jnp.where(top_left, dh, jnp.where(low_right, u2, jnp.where(left, d1, u1))),
                    jnp.where(top_left, d1, jnp.where(low_right, uh, jnp.where(left, d2, u2))),
                    jnp.where(left, dh, uh),
                ]
                fresh = []
                for i in range(len(o)):
                    s = src[indices[f], z, i]
                    a = jnp.exp(rates[f] * o[i])
                    mixed = (1.0 - TILT_SHARE) * states[f][i] + TILT_SHARE * winds[i]
                    fresh.append(s + a * (mixed - s))
                if last:
                    fresh.append(out)
                states[f] = tuple(fresh)
            for half in range(2):
                for f in range(BATCH):
                    acc[slots[f], z, half] = weights[f] * states[f][half]
        for f in range(BATCH):
            face_out[chunk, 0, f] = states[f][0]
            face_out[chunk, 1, f] = states[f][1]

        @pl.when(has_down)
        def _():
            main.start()

        @pl.when(has_down & has_right)
        def _():
            to_right.start()

        @pl.when(has_down & has_left)
        def _():
            to_left.start()

        for f in range(BATCH):
            acc[slots[f]] = acc[slots[f]] + acc[before[f]]
        return latest

    def group_step(k, latest):
        for sub in range(subs):
            latest = chunk_step(k, sub, latest)
        return tuple(latest)

    latest = lax.fori_loop(0, bands, group_step, (jnp.int32(0),) * LINES)

    beside = band + 1 - 2 * lax.rem(band, 2)
    across = lax.rem(band + 2, bands)
    corner = bands - 1 - band

    def gather_copy(kind, owner, zp, to):
        return pltpu.make_async_remote_copy(
            src_ref=gathered.at[owner, zp],
            dst_ref=gathered.at[owner, zp],
            send_sem=gat_send.at[kind, zp],
            recv_sem=gat_recv.at[kind, zp],
            device_id={"band": to},
            device_id_type=MESH,
        )

    def relax(zp, carry):
        for half in range(2):
            both = []
            for z in (zp, zp + pairs):
                p = COLLISION * plk[z, half]
                ratios = []
                for t in range(LINES):
                    j = acc[latest[t], z, half]
                    j = j + half_turn(j)
                    ratios.append((j + p) / ((1.0 + COLLISION) + j))
                one = 0.5 * (ratios[0] / ratios[2] + ratios[1] / ratios[3])
                levels = (one, ratios[1] / ratios[4], ratios[0], ratios[1])
                both.append(levels)
                scale = 1.0 / (1.0 + levels[0] + levels[1] + levels[2] + levels[3])
                rows = pl.ds(half * ROWS, ROWS)
                pops_out[0, z, rows] = scale[:, :HALF]
                for i in range(4):
                    pops_out[1 + i, z, rows] = (scale * levels[i])[:, :HALF]
            for i in range(4):
                gathered[band, zp, i, half] = jnp.where(left, both[0][i], both[1][i])
        gather_copy(0, band, zp, beside).start()
        gather_copy(1, band, zp, across).start()
        return carry

    for zp in range(pairs):
        relax(zp, 0)

    loads[6].wait()

    def forward(q, carry):
        gather_copy(0, beside, 2 * q, beside).wait_recv()
        gather_copy(2, beside, 2 * q, across).start()
        gather_copy(1, across, 2 * q + 1, across).wait_recv()
        gather_copy(2, across, 2 * q + 1, beside).start()
        return carry

    lax.fori_loop(0, pairs // 2, forward, 0)

    def finish_two(q, carry):
        gather_copy(1, across, 2 * q, across).wait_recv()
        gather_copy(2, corner, 2 * q, corner).wait_recv()
        finish(2 * q)
        gather_copy(0, beside, 2 * q + 1, beside).wait_recv()
        gather_copy(2, corner, 2 * q + 1, corner).wait_recv()
        finish(2 * q + 1)
        return carry

    def finish(zp):
        for pair in range(bands // 2):
            columns = slice(pair * LANES, (pair + 1) * LANES)
            for half in range(2):
                rows = pl.ds(half * ROWS, ROWS)
                lines = []
                for b in (2 * pair, 2 * pair + 1):
                    levels = [1.0] + [gathered[b, zp, i, half] for i in range(4)]
                    lines.append(
                        [
                            levels[UPPER_LEVEL[t]] / (levels[LOWER_LEVEL[t]] + levels[UPPER_LEVEL[t]])
                            for t in range(LINES)
                        ]
                    )
                first = EPS_THERMAL * planck_all[zp, rows, columns]
                second = EPS_THERMAL * planck_all[zp + pairs, rows, columns]
                for t in range(LINES):
                    even, odd = lines[0][t], lines[1][t]
                    new_src[t, zp, rows, columns] = first + (1.0 - EPS_THERMAL) * jnp.where(
                        left, even, half_turn(odd)
                    )
                    new_src[t, zp + pairs, rows, columns] = second + (
                        1.0 - EPS_THERMAL
                    ) * jnp.where(left, half_turn(even), odd)
        for f in range(freqs):
            t = line_index[f]
            source_out[f, zp] = new_src[t, zp]
            source_out[f, zp + pairs] = new_src[t, zp + pairs]

    lax.fori_loop(0, pairs // 2, finish_two, 0)

    for k in range(1, bands):
        for copy in par_copies(k):
            copy.wait_send()

    @pl.when(has_right)
    def _():
        halo_copy(0).wait_send()

    @pl.when(has_left)
    def _():
        halo_copy(1).wait_send()

    def drain(chunk, carry):
        main, to_right, to_left = face_copies(chunk)

        @pl.when(has_down)
        def _():
            main.wait_send()

        @pl.when(has_down & has_right)
        def _():
            to_right.wait_send()

        @pl.when(has_down & has_left)
        def _():
            to_left.wait_send()

        return carry

    lax.fori_loop(0, bands * subs, drain, 0)

    def drain_gather(zp, carry):
        gather_copy(0, band, zp, beside).wait_send()
        gather_copy(1, band, zp, across).wait_send()
        gather_copy(2, corner, zp, across).wait_send()
        return carry

    lax.fori_loop(0, pairs, drain_gather, 0)


def write_out(pops, source, pops_hbm, source_hbm, sem):
    copies = [pltpu.make_async_copy(pops, pops_hbm, sem.at[0])]
    for f in range(source.shape[0]):
        copies.append(pltpu.make_async_copy(source.at[f], source_hbm.at[f], sem.at[1 + f]))
    for copy in copies:
        copy.start()
    for copy in copies:
        copy.wait()


def per_device(sizes, strength, opacity, planck, old_populations, line_index, line_weight):
    bands, tiles, slabs = sizes
    depth, rows, cells = opacity.shape
    freqs = strength.shape[0]
    pairs = depth // 2
    chunks = bands * freqs // BATCH
    assert rows == 2 * ROWS and depth == ROWS and cells == bands * HALF and bands == 4
    f32 = jnp.float32
    hbm = pl.BlockSpec(memory_space=pltpu.HBM)
    vmem = pl.BlockSpec(memory_space=pltpu.VMEM)
    sem = pltpu.SemaphoreType.DMA
    tile = (ROWS, LANES)
    pops, source = pl.pallas_call(
        functools.partial(kernel, (bands, tiles, slabs, depth, freqs)),
        out_shape=(
            jax.ShapeDtypeStruct((LEVELS, depth, rows, cells // bands), f32),
            jax.ShapeDtypeStruct((freqs, depth, rows, cells), f32),
        ),
        in_specs=[hbm] * 6,
        out_specs=(vmem, vmem),
        scratch_shapes=[
            pltpu.SMEM((freqs,), f32),
            pltpu.SMEM((freqs,), jnp.int32),
            pltpu.SMEM((freqs,), f32),
            pltpu.VMEM((2 + LEVELS, depth, rows, LANES), f32),
            pltpu.VMEM((depth, rows, cells), f32),
            pltpu.VMEM((bands, 2) + tile, f32),
            pltpu.VMEM((bands, 1, LANES), jnp.int32),
            pltpu.SMEM((bands, 1, LANES), jnp.int32),
            pltpu.VMEM((2, 1 + LINES, pairs // 2) + tile, f32),
            pltpu.VMEM((2, 1 + LINES, pairs // 2) + tile, f32),
            pltpu.VMEM((depth, 3) + tile, f32),
            pltpu.VMEM((LINES, depth, 3) + tile, f32),
            pltpu.VMEM((depth, 2) + tile, f32),
            pltpu.VMEM((chunks, 2, BATCH) + tile, f32),
            pltpu.VMEM((2, chunks, BATCH) + tile, f32),
            pltpu.VMEM((chunks, 2, BATCH) + tile, f32),
            pltpu.VMEM((1 + bands * freqs, depth, 2) + tile, f32),
            pltpu.VMEM((bands, pairs, 4, 2) + tile, f32),
            pltpu.VMEM((LINES, depth, rows, cells), f32),
            sem((7,)),
            sem,
            sem((2, bands)),
            sem((2, bands)),
            sem((2,)),
            sem((2,)),
            sem((3, chunks)),
            sem((3, chunks)),
            sem((3, pairs)),
            sem((3, pairs)),
        ],
        compiler_params=pltpu.CompilerParams(
            collective_id=0, has_side_effects=True, vmem_limit_bytes=32 * 1024 * 1024
        ),
        cost_estimate=pl.CostEstimate(
            flops=60 * depth * rows * cells * freqs,
            bytes_accessed=16 * depth * rows * cells * 4,
            transcendentals=2 * depth * rows * cells * freqs,
        ),
    )(
        *(
            pltpu.with_memory_space_constraint(v, pltpu.HBM)
            for v in (strength, line_index, line_weight, opacity, planck, old_populations)
        )
    )
    return pl.pallas_call(
        write_out,
        out_shape=(
            jax.ShapeDtypeStruct(pops.shape, f32),
            jax.ShapeDtypeStruct(source.shape, f32),
        ),
        in_specs=[vmem] * 2,
        out_specs=(hbm, hbm),
        scratch_shapes=[sem((1 + freqs,))],
    )(
        pltpu.with_memory_space_constraint(pops, pltpu.VMEM),
        pltpu.with_memory_space_constraint(source, pltpu.VMEM),
    )


def solution(mesh):
    sizes = (mesh.shape["band"], mesh.shape["tile"], mesh.shape["slab"])
    in_specs = (
        P("band"),
        P("slab", "tile", None),
        P("slab", "tile", None),
        P(None, "slab", "tile", None),
        P("band"),
        P("band"),
    )
    out_specs = (P(None, "slab", "tile", "band"), P("band", "slab", "tile", None))
    return jax.shard_map(
        functools.partial(per_device, sizes),
        mesh=mesh,
        in_specs=in_specs,
        out_specs=out_specs,
        check_vma=False,
    )
```

```python
import functools

import jax
import jax.numpy as jnp
from jax import lax
from jax.experimental import pallas as pl
from jax.experimental.pallas import tpu as pltpu
from jax.sharding import PartitionSpec as P

MESH = pl.DeviceIdType.MESH
LINES = 5
LEVELS = 5
EPS_THERMAL = 0.1
COLLISION = 0.5
PATH_FACTOR = 1.25
TILT_SHARE = 0.4
LOWER_LEVEL = (0, 0, 1, 1, 2)
UPPER_LEVEL = (3, 4, 3, 4, 4)
LANES = 128
ROWS = 8
HALF = LANES // 2
BATCH = 8


def half_turn(v):
    return pltpu.roll(v, HALF, 1)


def kernel(
    sizes,
    strength_hbm,
    line_index_hbm,
    line_weight_hbm,
    opacity,
    planck,
    populations,
    pops_out,
    source_out,
    strength,
    line_index,
    line_weight,
    fields,
    planck_all,
    par_f,
    par_i,
    par_s,
    halo_out,
    halo_in,
    opac,
    src,
    plk,
    face_in,
    face_halo,
    face_out,
    acc,
    gathered,
    new_src,
    in_sem,
    idx_sem,
    par_send,
    par_recv,
    halo_send,
    halo_recv,
    face_send,
    face_recv,
    gat_send,
    gat_recv,
):
    bands, tiles, slabs, depth, freqs = sizes
    pairs = depth // 2
    subs = freqs // BATCH
    band = lax.axis_index("band")
    tile = lax.axis_index("tile")
    slab = lax.axis_index("slab")
    has_left = tile > 0
    has_right = tile < tiles - 1
    has_up = slab > 0
    has_down = slab < slabs - 1

    column = pl.multiple_of((band // 2) * LANES, LANES)
    loads = [
        pltpu.make_async_copy(opacity.at[:, :, pl.ds(column, LANES)], fields.at[0], in_sem.at[0]),
        pltpu.make_async_copy(planck.at[:, :, pl.ds(column, LANES)], fields.at[1], in_sem.at[1]),
        pltpu.make_async_copy(
            populations.at[:, :, :, pl.ds(column, LANES)], fields.at[pl.ds(2, LEVELS)], in_sem.at[2]
        ),
        pltpu.make_async_copy(strength_hbm, strength, in_sem.at[3]),
        pltpu.make_async_copy(line_index_hbm, line_index, in_sem.at[4]),
        pltpu.make_async_copy(line_weight_hbm, line_weight, in_sem.at[5]),
        pltpu.make_async_copy(planck, planck_all, in_sem.at[6]),
    ]
    for load in loads:
        load.start()

    barrier = pltpu.get_barrier_semaphore()
    for k in range(1, bands):
        pl.semaphore_signal(
            barrier, inc=1, device_id={"band": lax.rem(band + k, bands)}, device_id_type=MESH
        )
    expected = jnp.int32(bands - 1)
    for dt in (-1, 0, 1):
        for ds in (-1, 0, 1):
            if dt == 0 and ds == 0:
                continue
            there = (tile + dt >= 0) & (tile + dt < tiles) & (slab + ds >= 0) & (slab + ds < slabs)

            @pl.when(there)
            def _():
                pl.semaphore_signal(
                    barrier,
                    inc=1,
                    device_id={"tile": tile + dt, "slab": slab + ds},
                    device_id_type=MESH,
                )

            expected = expected + there.astype(jnp.int32)

    row = lax.broadcasted_iota(jnp.int32, (ROWS, LANES), 0)
    lane = lax.broadcasted_iota(jnp.int32, (ROWS, LANES), 1)
    left = lane < HALF
    own = (lane // HALF) == lax.rem(band, 2)
    top_left = left & (row == 0)
    low_right = jnp.logical_not(left) & (row == ROWS - 1)

    @pl.when(jnp.logical_not(has_left))
    def _():
        halo_in[0] = jnp.zeros(halo_in.shape[1:], jnp.float32)
        face_halo[0] = jnp.zeros(face_halo.shape[1:], jnp.float32)

    @pl.when(jnp.logical_not(has_right))
    def _():
        halo_in[1] = jnp.zeros(halo_in.shape[1:], jnp.float32)
        face_halo[1] = jnp.zeros(face_halo.shape[1:], jnp.float32)

    @pl.when(jnp.logical_not(has_up))
    def _():
        face_in[...] = jnp.zeros(face_in.shape, jnp.float32)
        face_halo[...] = jnp.zeros(face_halo.shape, jnp.float32)

    acc[0] = jnp.zeros(acc.shape[1:], jnp.float32)

    def par_copies(k):
        to = {"band": lax.rem(band + k, bands)}
        return (
            pltpu.make_async_remote_copy(
                src_ref=par_f.at[0],
                dst_ref=par_f.at[k],
                send_sem=par_send.at[0, k],
                recv_sem=par_recv.at[0, k],
                device_id=to,
                device_id_type=MESH,
            ),
            pltpu.make_async_remote_copy(
                src_ref=par_i.at[0],
                dst_ref=par_i.at[k],
                send_sem=par_send.at[1, k],
                recv_sem=par_recv.at[1, k],
                device_id=to,
                device_id_type=MESH,
            ),
        )

    for load in loads[:6]:
        load.wait()

    lane_row = lax.broadcasted_iota(jnp.int32, (1, LANES), 1)
    indices = jnp.zeros((1, LANES), jnp.int32)
    zero = jnp.zeros((ROWS, LANES), jnp.float32)
    rate, weight = zero, zero
    for f in range(freqs):
        here = row == f
        rate = jnp.where(here, -PATH_FACTOR * strength[f], rate)
        weight = jnp.where(here, line_weight[f] * (LINES / (2.0 * freqs * bands)), weight)
        indices = jnp.where(lane_row == f, line_index[f], indices)
    par_f[0, 0] = rate
    par_f[0, 1] = weight
    par_i[0] = indices

    def spread(v):
        return jnp.where(own, v, half_turn(v))

    def prepare(z, carry):
        for half in range(2):
            rows = pl.ds(half * ROWS, ROWS)
            p = spread(fields[1, z, rows])
            levels = [spread(fields[2 + i, z, rows]) for i in range(LEVELS)]
            opac[z, half] = spread(fields[0, z, rows])
            plk[z, half] = p
            for t in range(LINES):
                low, up = levels[LOWER_LEVEL[t]], levels[UPPER_LEVEL[t]]
                src[t, z, half] = EPS_THERMAL * p + (1.0 - EPS_THERMAL) * (up / (low + up))
        return carry

    for z in range(depth):
        prepare(z, 0)

    def layer(i, z, part):
        return opac[z, part] if i == 0 else src[i - 1, z, part]

    for i in range(1 + LINES):
        right, down = [], []
        for z in range(pairs):
            y = depth - 2 - z
            a, b = layer(i, z, 1), layer(i, z, 0)
            if y > z:
                a = jnp.where(row >= 1 + z, a, pltpu.roll(layer(i, y, 1), z + 1, 0))
                b = jnp.where(row <= y, b, pltpu.roll(layer(i, y, 0), y + 1, 0))
            right.append(a)
            down.append(b)
        for q in range(pairs // 2):
            halo_out[0, i, q] = jnp.where(left, right[q], right[q + pairs // 2])
            halo_out[1, i, q] = jnp.where(left, down[q + pairs // 2], down[q])

    pl.semaphore_wait(barrier, expected)
    for k in range(1, bands):
        for copy in par_copies(k):
            copy.start()

    def halo_copy(side):
        return pltpu.make_async_remote_copy(
            src_ref=halo_out.at[side],
            dst_ref=halo_in.at[side],
            send_sem=halo_send.at[side],
            recv_sem=halo_recv.at[side],
            device_id={"tile": tile + (1 if side == 0 else -1)},
            device_id_type=MESH,
        )

    @pl.when(has_right)
    def _():
        halo_copy(0).start()

    @pl.when(has_left)
    def _():
        halo_copy(1).start()

    for k in range(1, bands):
        for copy in par_copies(k):
            copy.wait_recv()
    to_scalars = pltpu.make_async_copy(par_i, par_s, idx_sem)
    to_scalars.start()

    @pl.when(has_left)
    def _():
        halo_copy(0).wait_recv()

    @pl.when(has_right)
    def _():
        halo_copy(1).wait_recv()

    for i in range(1 + LINES):
        for q in range(pairs // 2):
            a, b = halo_in[0, i, q], halo_in[1, i, q]
            shared = {q: jnp.where(left, a, b)}
            shared[q + pairs // 2] = half_turn(jnp.where(left, b, a))
            for z, tile_rows in shared.items():
                y = depth - 2 - z
                both = [(z, tile_rows)]
                if y > z:
                    moved = (pltpu.roll(tile_rows, y + 1, 0), pltpu.roll(tile_rows, z + 1, 0))
                    both.append((y, jnp.where(left, *moved)))
                for at, v in both:
                    if i == 0:
                        opac[at, 2] = v
                    else:
                        src[i - 1, at, 2] = v

    to_scalars.wait()

    def face_copies(chunk):
        def make(part, source, target, to):
            return pltpu.make_async_remote_copy(
                src_ref=source,
                dst_ref=target,
                send_sem=face_send.at[part, chunk],
                recv_sem=face_recv.at[part, chunk],
                device_id=to,
                device_id_type=MESH,
            )

        return (
            make(0, face_out.at[chunk], face_in.at[chunk], {"slab": slab + 1}),
            make(
                1,
                face_out.at[chunk, 1],
                face_halo.at[0, chunk],
                {"tile": tile + 1, "slab": slab + 1},
            ),
            make(
                2,
                face_out.at[chunk, 0],
                face_halo.at[1, chunk],
                {"tile": tile - 1, "slab": slab + 1},
            ),
        )

    def chunk_step(k, sub, latest):
        chunk = k * subs + sub
        main, to_right, to_left = face_copies(chunk)

        @pl.when(has_up)
        def _():
            main.wait_recv()

        @pl.when(has_up & has_left)
        def _():
            to_right.wait_recv()

        @pl.when(has_up & has_right)
        def _():
            to_left.wait_recv()

        states, rates, weights, indices, before, slots = [], [], [], [], [], []
        for f in range(BATCH):
            at = pl.ds(sub * BATCH + f, 1)
            rates.append(jnp.broadcast_to(par_f[k, 0, at], (ROWS, LANES)))
            weights.append(jnp.broadcast_to(par_f[k, 1, at], (ROWS, LANES)))
            line = par_s[k, 0, sub * BATCH + f]
            indices.append(line)
            slot = k * freqs + (sub * BATCH + f + 1)
            previous = latest[0]
            for t in range(1, LINES):
                previous = jnp.where(line == t, latest[t], previous)
            latest = [jnp.where(line == t, slot, latest[t]) for t in range(LINES)]
            before.append(previous)
            slots.append(slot)
            beyond = jnp.where(left, face_halo[0, chunk, f], face_halo[1, chunk, f])
            states.append((face_in[chunk, 0, f], face_in[chunk, 1, f], beyond))
        for z in range(depth):
            last = z == depth - 1
            o = [opac[z, i] for i in range(2 if last else 3)]
            for f in range(BATCH):
                one, two, out = states[f]
                d1, d2, dh = (pltpu.roll(v, 1, 0) for v in (one, two, out))
                u1, u2, uh = (pltpu.roll(v, ROWS - 1, 0) for v in (one, two, out))
                winds = [
                    jnp.where(top_left, dh, jnp.where(low_right, u2, jnp.where(left, d1, u1))),
                    jnp.where(top_left, d1, jnp.where(low_right, uh, jnp.where(left, d2, u2))),
                    jnp.where(left, dh, uh),
                ]
                fresh = []
                for i in range(len(o)):
                    s = src[indices[f], z, i]
                    a = jnp.exp(rates[f] * o[i])
                    mixed = (1.0 - TILT_SHARE) * states[f][i] + TILT_SHARE * winds[i]
                    fresh.append(s + a * (mixed - s))
                if last:
                    fresh.append(out)
                states[f] = tuple(fresh)
            for half in range(2):
                for f in range(BATCH):
                    acc[slots[f], z, half] = weights[f] * states[f][half]
        for f in range(BATCH):
            face_out[chunk, 0, f] = states[f][0]
            face_out[chunk, 1, f] = states[f][1]

        @pl.when(has_down)
        def _():
            main.start()

        @pl.when(has_down & has_right)
        def _():
            to_right.start()

        @pl.when(has_down & has_left)
        def _():
            to_left.start()

        for f in range(BATCH):
            acc[slots[f]] = acc[slots[f]] + acc[before[f]]
        return latest

    def group_step(k, latest):
        for sub in range(subs):
            latest = chunk_step(k, sub, latest)
        return tuple(latest)

    latest = lax.fori_loop(0, bands, group_step, (jnp.int32(0),) * LINES)

    beside = band + 1 - 2 * lax.rem(band, 2)
    across = lax.rem(band + 2, bands)
    corner = bands - 1 - band

    def gather_copy(kind, owner, zp, to):
        return pltpu.make_async_remote_copy(
            src_ref=gathered.at[owner, zp],
            dst_ref=gathered.at[owner, zp],
            send_sem=gat_send.at[kind, zp],
            recv_sem=gat_recv.at[kind, zp],
            device_id={"band": to},
            device_id_type=MESH,
        )

    def relax(zp, carry):
        for half in range(2):
            both = []
            for z in (zp, zp + pairs):
                p = COLLISION * plk[z, half]
                ratios = []
                for t in range(LINES):
                    j = acc[latest[t], z, half]
                    j = j + half_turn(j)
                    ratios.append((j + p) / ((1.0 + COLLISION) + j))
                one = 0.5 * (ratios[0] / ratios[2] + ratios[1] / ratios[3])
                levels = (one, ratios[1] / ratios[4], ratios[0], ratios[1])
                both.append(levels)
            for i in range(4):
                gathered[band, zp, i, half] = jnp.where(left, both[0][i], both[1][i])
        gather_copy(0, band, zp, beside).start()
        gather_copy(1, band, zp, across).start()
        return carry

    for zp in range(pairs):
        relax(zp, 0)

    loads[6].wait()

    def forward(q, carry):
        gather_copy(0, beside, 2 * q, beside).wait_recv()
        gather_copy(2, beside, 2 * q, across).start()
        gather_copy(1, across, 2 * q + 1, across).wait_recv()
        gather_copy(2, across, 2 * q + 1, beside).start()
        return carry

    lax.fori_loop(0, pairs // 2, forward, 0)

    def normalise(zp, carry):
        for half in range(2):
            rows = pl.ds(half * ROWS, ROWS)
            levels = [gathered[band, zp, i, half] for i in range(4)]
            scale = 1.0 / (1.0 + levels[0] + levels[1] + levels[2] + levels[3])
            for i, v in enumerate([scale] + [scale * level for level in levels]):
                pops_out[i, zp, rows] = v[:, :HALF]
                pops_out[i, zp + pairs, rows] = half_turn(v)[:, :HALF]
        return carry

    lax.fori_loop(0, pairs, normalise, 0)

    def finish_two(q, carry):
        gather_copy(1, across, 2 * q, across).wait_recv()
        gather_copy(2, corner, 2 * q, corner).wait_recv()
        finish(2 * q)
        gather_copy(0, beside, 2 * q + 1, beside).wait_recv()
        gather_copy(2, corner, 2 * q + 1, corner).wait_recv()
        finish(2 * q + 1)
        return carry

    def finish(zp):
        for pair in range(bands // 2):
            columns = slice(pair * LANES, (pair + 1) * LANES)
            for half in range(2):
                rows = pl.ds(half * ROWS, ROWS)
                lines = []
                for b in (2 * pair, 2 * pair + 1):
                    levels = [1.0] + [gathered[b, zp, i, half] for i in range(4)]
                    lines.append(
                        [
                            levels[UPPER_LEVEL[t]] / (levels[LOWER_LEVEL[t]] + levels[UPPER_LEVEL[t]])
                            for t in range(LINES)
                        ]
                    )
                first = EPS_THERMAL * planck_all[zp, rows, columns]
                second = EPS_THERMAL * planck_all[zp + pairs, rows, columns]
                for t in range(LINES):
                    even, odd = lines[0][t], lines[1][t]
                    new_src[t, zp, rows, columns] = first + (1.0 - EPS_THERMAL) * jnp.where(
                        left, even, half_turn(odd)
                    )
                    new_src[t, zp + pairs, rows, columns] = second + (
                        1.0 - EPS_THERMAL
                    ) * jnp.where(left, half_turn(even), odd)
        for f in range(freqs):
            t = line_index[f]
            source_out[f, zp] = new_src[t, zp]
            source_out[f, zp + pairs] = new_src[t, zp + pairs]

    lax.fori_loop(0, pairs // 2, finish_two, 0)

    for k in range(1, bands):
        for copy in par_copies(k):
            copy.wait_send()

    @pl.when(has_right)
    def _():
        halo_copy(0).wait_send()

    @pl.when(has_left)
    def _():
        halo_copy(1).wait_send()

    def drain(chunk, carry):
        main, to_right, to_left = face_copies(chunk)

        @pl.when(has_down)
        def _():
            main.wait_send()

        @pl.when(has_down & has_right)
        def _():
            to_right.wait_send()

        @pl.when(has_down & has_left)
        def _():
            to_left.wait_send()

        return carry

    lax.fori_loop(0, bands * subs, drain, 0)

    def drain_gather(zp, carry):
        gather_copy(0, band, zp, beside).wait_send()
        gather_copy(1, band, zp, across).wait_send()
        gather_copy(2, corner, zp, across).wait_send()
        return carry

    lax.fori_loop(0, pairs, drain_gather, 0)


def write_out(pops, source, pops_hbm, source_hbm, sem):
    copies = [pltpu.make_async_copy(pops, pops_hbm, sem.at[0])]
    for f in range(source.shape[0]):
        copies.append(pltpu.make_async_copy(source.at[f], source_hbm.at[f], sem.at[1 + f]))
    for copy in copies:
        copy.start()
    for copy in copies:
        copy.wait()


def per_device(sizes, strength, opacity, planck, old_populations, line_index, line_weight):
    bands, tiles, slabs = sizes
    depth, rows, cells = opacity.shape
    freqs = strength.shape[0]
    pairs = depth // 2
    chunks = bands * freqs // BATCH
    assert rows == 2 * ROWS and depth == ROWS and cells == bands * HALF and bands == 4
    f32 = jnp.float32
    hbm = pl.BlockSpec(memory_space=pltpu.HBM)
    vmem = pl.BlockSpec(memory_space=pltpu.VMEM)
    sem = pltpu.SemaphoreType.DMA
    tile = (ROWS, LANES)
    pops, source = pl.pallas_call(
        functools.partial(kernel, (bands, tiles, slabs, depth, freqs)),
        out_shape=(
            jax.ShapeDtypeStruct((LEVELS, depth, rows, cells // bands), f32),
            jax.ShapeDtypeStruct((freqs, depth, rows, cells), f32),
        ),
        in_specs=[hbm] * 6,
        out_specs=(vmem, vmem),
        scratch_shapes=[
            pltpu.SMEM((freqs,), f32),
            pltpu.SMEM((freqs,), jnp.int32),
            pltpu.SMEM((freqs,), f32),
            pltpu.VMEM((2 + LEVELS, depth, rows, LANES), f32),
            pltpu.VMEM((depth, rows, cells), f32),
            pltpu.VMEM((bands, 2) + tile, f32),
            pltpu.VMEM((bands, 1, LANES), jnp.int32),
            pltpu.SMEM((bands, 1, LANES), jnp.int32),
            pltpu.VMEM((2, 1 + LINES, pairs // 2) + tile, f32),
            pltpu.VMEM((2, 1 + LINES, pairs // 2) + tile, f32),
            pltpu.VMEM((depth, 3) + tile, f32),
            pltpu.VMEM((LINES, depth, 3) + tile, f32),
            pltpu.VMEM((depth, 2) + tile, f32),
            pltpu.VMEM((chunks, 2, BATCH) + tile, f32),
            pltpu.VMEM((2, chunks, BATCH) + tile, f32),
            pltpu.VMEM((chunks, 2, BATCH) + tile, f32),
            pltpu.VMEM((1 + bands * freqs, depth, 2) + tile, f32),
            pltpu.VMEM((bands, pairs, 4, 2) + tile, f32),
            pltpu.VMEM((LINES, depth, rows, cells), f32),
            sem((7,)),
            sem,
            sem((2, bands)),
            sem((2, bands)),
            sem((2,)),
            sem((2,)),
            sem((3, chunks)),
            sem((3, chunks)),
            sem((3, pairs)),
            sem((3, pairs)),
        ],
        compiler_params=pltpu.CompilerParams(
            collective_id=0, has_side_effects=True, vmem_limit_bytes=32 * 1024 * 1024
        ),
        cost_estimate=pl.CostEstimate(
            flops=60 * depth * rows * cells * freqs,
            bytes_accessed=16 * depth * rows * cells * 4,
            transcendentals=2 * depth * rows * cells * freqs,
        ),
    )(
        *(
            pltpu.with_memory_space_constraint(v, pltpu.HBM)
            for v in (strength, line_index, line_weight, opacity, planck, old_populations)
        )
    )
    return pl.pallas_call(
        write_out,
        out_shape=(
            jax.ShapeDtypeStruct(pops.shape, f32),
            jax.ShapeDtypeStruct(source.shape, f32),
        ),
        in_specs=[vmem] * 2,
        out_specs=(hbm, hbm),
        scratch_shapes=[sem((1 + freqs,))],
    )(
        pltpu.with_memory_space_constraint(pops, pltpu.VMEM),
        pltpu.with_memory_space_constraint(source, pltpu.VMEM),
    )


def solution(mesh):
    sizes = (mesh.shape["band"], mesh.shape["tile"], mesh.shape["slab"])
    in_specs = (
        P("band"),
        P("slab", "tile", None),
        P("slab", "tile", None),
        P(None, "slab", "tile", None),
        P("band"),
        P("band"),
    )
    out_specs = (P(None, "slab", "tile", "band"), P("band", "slab", "tile", None))
    return jax.shard_map(
        functools.partial(per_device, sizes),
        mesh=mesh,
        in_specs=in_specs,
        out_specs=out_specs,
        check_vma=False,
    )
```

```python
import functools

import jax
import jax.numpy as jnp
from jax import lax
from jax.experimental import pallas as pl
from jax.experimental.pallas import tpu as pltpu
from jax.sharding import PartitionSpec as P

MESH = pl.DeviceIdType.MESH
LINES = 5
LEVELS = 5
EPS_THERMAL = 0.1
COLLISION = 0.5
PATH_FACTOR = 1.25
TILT_SHARE = 0.4
LOWER_LEVEL = (0, 0, 1, 1, 2)
UPPER_LEVEL = (3, 4, 3, 4, 4)
LANES = 128
ROWS = 8
HALF = LANES // 2
BATCH = 8


def half_turn(v):
    return pltpu.roll(v, HALF, 1)


def kernel(
    sizes,
    strength_hbm,
    line_index_hbm,
    line_weight_hbm,
    opacity,
    planck,
    populations,
    pops_out,
    source_out,
    strength,
    line_index,
    line_weight,
    fields,
    planck_all,
    par_f,
    par_i,
    par_s,
    halo_out,
    halo_in,
    opac,
    src,
    plk,
    face_in,
    face_halo,
    face_out,
    acc,
    gathered,
    new_src,
    in_sem,
    idx_sem,
    par_send,
    par_recv,
    halo_send,
    halo_recv,
    face_send,
    face_recv,
    gat_send,
    gat_recv,
):
    bands, tiles, slabs, depth, freqs = sizes
    pairs = depth // 2
    subs = freqs // BATCH
    band = lax.axis_index("band")
    tile = lax.axis_index("tile")
    slab = lax.axis_index("slab")
    has_left = tile > 0
    has_right = tile < tiles - 1
    has_up = slab > 0
    has_down = slab < slabs - 1

    column = pl.multiple_of((band // 2) * LANES, LANES)
    loads = [
        pltpu.make_async_copy(opacity.at[:, :, pl.ds(column, LANES)], fields.at[0], in_sem.at[0]),
        pltpu.make_async_copy(planck.at[:, :, pl.ds(column, LANES)], fields.at[1], in_sem.at[1]),
        pltpu.make_async_copy(
            populations.at[:, :, :, pl.ds(column, LANES)], fields.at[pl.ds(2, LEVELS)], in_sem.at[2]
        ),
        pltpu.make_async_copy(strength_hbm, strength, in_sem.at[3]),
        pltpu.make_async_copy(line_index_hbm, line_index, in_sem.at[4]),
        pltpu.make_async_copy(line_weight_hbm, line_weight, in_sem.at[5]),
        pltpu.make_async_copy(planck, planck_all, in_sem.at[6]),
    ]
    for load in loads:
        load.start()

    barrier = pltpu.get_barrier_semaphore()
    for k in range(1, bands):
        pl.semaphore_signal(
            barrier, inc=1, device_id={"band": lax.rem(band + k, bands)}, device_id_type=MESH
        )
    expected = jnp.int32(bands - 1)
    for dt in (-1, 0, 1):
        for ds in (-1, 0, 1):
            if dt == 0 and ds == 0:
                continue
            there = (tile + dt >= 0) & (tile + dt < tiles) & (slab + ds >= 0) & (slab + ds < slabs)

            @pl.when(there)
            def _():
                pl.semaphore_signal(
                    barrier,
                    inc=1,
                    device_id={"tile": tile + dt, "slab": slab + ds},
                    device_id_type=MESH,
                )

            expected = expected + there.astype(jnp.int32)

    row = lax.broadcasted_iota(jnp.int32, (ROWS, LANES), 0)
    lane = lax.broadcasted_iota(jnp.int32, (ROWS, LANES), 1)
    left = lane < HALF
    own = (lane // HALF) == lax.rem(band, 2)
    top_left = left & (row == 0)
    low_right = jnp.logical_not(left) & (row == ROWS - 1)

    @pl.when(jnp.logical_not(has_left))
    def _():
        halo_in[0] = jnp.zeros(halo_in.shape[1:], jnp.float32)
        face_halo[0] = jnp.zeros(face_halo.shape[1:], jnp.float32)

    @pl.when(jnp.logical_not(has_right))
    def _():
        halo_in[1] = jnp.zeros(halo_in.shape[1:], jnp.float32)
        face_halo[1] = jnp.zeros(face_halo.shape[1:], jnp.float32)

    @pl.when(jnp.logical_not(has_up))
    def _():
        face_in[...] = jnp.zeros(face_in.shape, jnp.float32)
        face_halo[...] = jnp.zeros(face_halo.shape, jnp.float32)

    acc[0] = jnp.zeros(acc.shape[1:], jnp.float32)

    def par_copies(k):
        to = {"band": lax.rem(band + k, bands)}
        return (
            pltpu.make_async_remote_copy(
                src_ref=par_f.at[0],
                dst_ref=par_f.at[k],
                send_sem=par_send.at[0, k],
                recv_sem=par_recv.at[0, k],
                device_id=to,
                device_id_type=MESH,
            ),
            pltpu.make_async_remote_copy(
                src_ref=par_i.at[0],
                dst_ref=par_i.at[k],
                send_sem=par_send.at[1, k],
                recv_sem=par_recv.at[1, k],
                device_id=to,
                device_id_type=MESH,
            ),
        )

    for load in loads[:6]:
        load.wait()

    lane_row = lax.broadcasted_iota(jnp.int32, (1, LANES), 1)
    indices = jnp.zeros((1, LANES), jnp.int32)
    zero = jnp.zeros((ROWS, LANES), jnp.float32)
    rate, weight = zero, zero
    for f in range(freqs):
        here = row == f
        rate = jnp.where(here, -PATH_FACTOR * strength[f], rate)
        weight = jnp.where(here, line_weight[f] * (LINES / (2.0 * freqs * bands)), weight)
        indices = jnp.where(lane_row == f, line_index[f], indices)
    par_f[0, 0] = rate
    par_f[0, 1] = weight
    par_i[0] = indices

    def spread(v):
        return jnp.where(own, v, half_turn(v))

    def prepare(z, carry):
        for half in range(2):
            rows = pl.ds(half * ROWS, ROWS)
            p = spread(fields[1, z, rows])
            levels = [spread(fields[2 + i, z, rows]) for i in range(LEVELS)]
            opac[z, half] = spread(fields[0, z, rows])
            plk[z, half] = p
            for t in range(LINES):
                low, up = levels[LOWER_LEVEL[t]], levels[UPPER_LEVEL[t]]
                src[t, z, half] = EPS_THERMAL * p + (1.0 - EPS_THERMAL) * (up / (low + up))
        return carry

    for z in range(depth):
        prepare(z, 0)

    def layer(i, z, part):
        return opac[z, part] if i == 0 else src[i - 1, z, part]

    for i in range(1 + LINES):
        right, down = [], []
        for z in range(pairs):
            y = depth - 2 - z
            a, b = layer(i, z, 1), layer(i, z, 0)
            if y > z:
                a = jnp.where(row >= 1 + z, a, pltpu.roll(layer(i, y, 1), z + 1, 0))
                b = jnp.where(row <= y, b, pltpu.roll(layer(i, y, 0), y + 1, 0))
            right.append(a)
            down.append(b)
        for q in range(pairs // 2):
            halo_out[0, i, q] = jnp.where(left, right[q], right[q + pairs // 2])
            halo_out[1, i, q] = jnp.where(left, down[q + pairs // 2], down[q])

    pl.semaphore_wait(barrier, expected)
    for k in range(1, bands):
        for copy in par_copies(k):
            copy.start()

    def halo_copy(side):
        return pltpu.make_async_remote_copy(
            src_ref=halo_out.at[side],
            dst_ref=halo_in.at[side],
            send_sem=halo_send.at[side],
            recv_sem=halo_recv.at[side],
            device_id={"tile": tile + (1 if side == 0 else -1)},
            device_id_type=MESH,
        )

    @pl.when(has_right)
    def _():
        halo_copy(0).start()

    @pl.when(has_left)
    def _():
        halo_copy(1).start()

    for k in range(1, bands):
        for copy in par_copies(k):
            copy.wait_recv()
    to_scalars = pltpu.make_async_copy(par_i, par_s, idx_sem)
    to_scalars.start()

    @pl.when(has_left)
    def _():
        halo_copy(0).wait_recv()

    @pl.when(has_right)
    def _():
        halo_copy(1).wait_recv()

    for i in range(1 + LINES):
        for q in range(pairs // 2):
            a, b = halo_in[0, i, q], halo_in[1, i, q]
            shared = {q: jnp.where(left, a, b)}
            shared[q + pairs // 2] = half_turn(jnp.where(left, b, a))
            for z, tile_rows in shared.items():
                y = depth - 2 - z
                both = [(z, tile_rows)]
                if y > z:
                    moved = (pltpu.roll(tile_rows, y + 1, 0), pltpu.roll(tile_rows, z + 1, 0))
                    both.append((y, jnp.where(left, *moved)))
                for at, v in both:
                    if i == 0:
                        opac[at, 2] = v
                    else:
                        src[i - 1, at, 2] = v

    to_scalars.wait()

    def face_copies(chunk):
        def make(part, source, target, to):
            return pltpu.make_async_remote_copy(
                src_ref=source,
                dst_ref=target,
                send_sem=face_send.at[part, chunk],
                recv_sem=face_recv.at[part, chunk],
                device_id=to,
                device_id_type=MESH,
            )

        return (
            make(0, face_out.at[chunk], face_in.at[chunk], {"slab": slab + 1}),
            make(
                1,
                face_out.at[chunk, 1],
                face_halo.at[0, chunk],
                {"tile": tile + 1, "slab": slab + 1},
            ),
            make(
                2,
                face_out.at[chunk, 0],
                face_halo.at[1, chunk],
                {"tile": tile - 1, "slab": slab + 1},
            ),
        )

    def chunk_step(k, sub, latest):
        chunk = k * subs + sub
        main, to_right, to_left = face_copies(chunk)

        @pl.when(has_up)
        def _():
            main.wait_recv()

        @pl.when(has_up & has_left)
        def _():
            to_right.wait_recv()

        @pl.when(has_up & has_right)
        def _():
            to_left.wait_recv()

        states, rates, weights, indices, before, slots = [], [], [], [], [], []
        for f in range(BATCH):
            at = pl.ds(sub * BATCH + f, 1)
            rates.append(jnp.broadcast_to(par_f[k, 0, at], (ROWS, LANES)))
            weights.append(jnp.broadcast_to(par_f[k, 1, at], (ROWS, LANES)))
            line = par_s[k, 0, sub * BATCH + f]
            indices.append(line)
            slot = k * freqs + (sub * BATCH + f + 1)
            previous = latest[0]
            for t in range(1, LINES):
                previous = jnp.where(line == t, latest[t], previous)
            latest = [jnp.where(line == t, slot, latest[t]) for t in range(LINES)]
            before.append(previous)
            slots.append(slot)
            beyond = jnp.where(left, face_halo[0, chunk, f], face_halo[1, chunk, f])
            states.append((face_in[chunk, 0, f], face_in[chunk, 1, f], beyond))
        for z in range(depth):
            last = z == depth - 1
            o = [opac[z, i] for i in range(2 if last else 3)]
            for f in range(BATCH):
                one, two, out = states[f]
                d1, d2, dh = (pltpu.roll(v, 1, 0) for v in (one, two, out))
                u1, u2, uh = (pltpu.roll(v, ROWS - 1, 0) for v in (one, two, out))
                winds = [
                    jnp.where(top_left, dh, jnp.where(low_right, u2, jnp.where(left, d1, u1))),
                    jnp.where(top_left, d1, jnp.where(low_right, uh, jnp.where(left, d2, u2))),
                    jnp.where(left, dh, uh),
                ]
                fresh = []
                for i in range(len(o)):
                    s = src[indices[f], z, i]
                    a = jnp.exp(rates[f] * o[i])
                    mixed = (1.0 - TILT_SHARE) * states[f][i] + TILT_SHARE * winds[i]
                    fresh.append(s + a * (mixed - s))
                if last:
                    fresh.append(out)
                states[f] = tuple(fresh)
            for half in range(2):
                for f in range(BATCH):
                    acc[slots[f], z, half] = weights[f] * states[f][half]
        for f in range(BATCH):
            face_out[chunk, 0, f] = states[f][0]
            face_out[chunk, 1, f] = states[f][1]

        @pl.when(has_down)
        def _():
            main.start()

        @pl.when(has_down & has_right)
        def _():
            to_right.start()

        @pl.when(has_down & has_left)
        def _():
            to_left.start()

        for f in range(BATCH):
            acc[slots[f]] = acc[slots[f]] + acc[before[f]]
        return latest

    def group_step(k, latest):
        for sub in range(subs):
            latest = chunk_step(k, sub, latest)
        return tuple(latest)

    latest = lax.fori_loop(0, bands, group_step, (jnp.int32(0),) * LINES)

    beside = band + 1 - 2 * lax.rem(band, 2)
    across = lax.rem(band + 2, bands)
    corner = bands - 1 - band

    def gather_copy(kind, owner, zp, to):
        return pltpu.make_async_remote_copy(
            src_ref=gathered.at[owner, zp],
            dst_ref=gathered.at[owner, zp],
            send_sem=gat_send.at[kind, zp],
            recv_sem=gat_recv.at[kind, zp],
            device_id={"band": to},
            device_id_type=MESH,
        )

    def relax(zp, carry):
        for half in range(2):
            both = []
            for z in (zp, zp + pairs):
                p = COLLISION * plk[z, half]
                ratios = []
                for t in range(LINES):
                    j = acc[latest[t], z, half]
                    j = j + half_turn(j)
                    ratios.append((j + p) / ((1.0 + COLLISION) + j))
                one = 0.5 * (ratios[0] / ratios[2] + ratios[1] / ratios[3])
                levels = (one, ratios[1] / ratios[4], ratios[0], ratios[1])
                both.append(levels)
            for i in range(4):
                gathered[band, zp, i, half] = jnp.where(left, both[0][i], both[1][i])
        gather_copy(0, band, zp, beside).start()
        gather_copy(1, band, zp, across).start()
        gather_copy(2, band, zp, corner).start()
        return carry

    for zp in range(pairs):
        relax(zp, 0)

    loads[6].wait()

    def normalise(zp, carry):
        for half in range(2):
            rows = pl.ds(half * ROWS, ROWS)
            levels = [gathered[band, zp, i, half] for i in range(4)]
            scale = 1.0 / (1.0 + levels[0] + levels[1] + levels[2] + levels[3])
            for i, v in enumerate([scale] + [scale * level for level in levels]):
                pops_out[i, zp, rows] = v[:, :HALF]
                pops_out[i, zp + pairs, rows] = half_turn(v)[:, :HALF]
        return carry

    lax.fori_loop(0, pairs, normalise, 0)

    def finish_two(q, carry):
        gather_copy(0, beside, 2 * q, beside).wait_recv()
        gather_copy(1, across, 2 * q, across).wait_recv()
        gather_copy(2, corner, 2 * q, corner).wait_recv()
        finish(2 * q)
        gather_copy(0, beside, 2 * q + 1, beside).wait_recv()
        gather_copy(1, across, 2 * q + 1, across).wait_recv()
        gather_copy(2, corner, 2 * q + 1, corner).wait_recv()
        finish(2 * q + 1)
        return carry

    def finish(zp):
        for pair in range(bands // 2):
            columns = slice(pair * LANES, (pair + 1) * LANES)
            for half in range(2):
                rows = pl.ds(half * ROWS, ROWS)
                lines = []
                for b in (2 * pair, 2 * pair + 1):
                    levels = [1.0] + [gathered[b, zp, i, half] for i in range(4)]
                    lines.append(
                        [
                            levels[UPPER_LEVEL[t]] / (levels[LOWER_LEVEL[t]] + levels[UPPER_LEVEL[t]])
                            for t in range(LINES)
                        ]
                    )
                first = EPS_THERMAL * planck_all[zp, rows, columns]
                second = EPS_THERMAL * planck_all[zp + pairs, rows, columns]
                for t in range(LINES):
                    even, odd = lines[0][t], lines[1][t]
                    new_src[t, zp, rows, columns] = first + (1.0 - EPS_THERMAL) * jnp.where(
                        left, even, half_turn(odd)
                    )
                    new_src[t, zp + pairs, rows, columns] = second + (
                        1.0 - EPS_THERMAL
                    ) * jnp.where(left, half_turn(even), odd)
        for f in range(freqs):
            t = line_index[f]
            source_out[f, zp] = new_src[t, zp]
            source_out[f, zp + pairs] = new_src[t, zp + pairs]

    lax.fori_loop(0, pairs // 2, finish_two, 0)

    for k in range(1, bands):
        for copy in par_copies(k):
            copy.wait_send()

    @pl.when(has_right)
    def _():
        halo_copy(0).wait_send()

    @pl.when(has_left)
    def _():
        halo_copy(1).wait_send()

    def drain(chunk, carry):
        main, to_right, to_left = face_copies(chunk)

        @pl.when(has_down)
        def _():
            main.wait_send()

        @pl.when(has_down & has_right)
        def _():
            to_right.wait_send()

        @pl.when(has_down & has_left)
        def _():
            to_left.wait_send()

        return carry

    lax.fori_loop(0, bands * subs, drain, 0)

    def drain_gather(zp, carry):
        gather_copy(0, band, zp, beside).wait_send()
        gather_copy(1, band, zp, across).wait_send()
        gather_copy(2, band, zp, corner).wait_send()
        return carry

    lax.fori_loop(0, pairs, drain_gather, 0)


def write_out(pops, source, pops_hbm, source_hbm, sem):
    copies = [pltpu.make_async_copy(pops, pops_hbm, sem.at[0])]
    for f in range(source.shape[0]):
        copies.append(pltpu.make_async_copy(source.at[f], source_hbm.at[f], sem.at[1 + f]))
    for copy in copies:
        copy.start()
    for copy in copies:
        copy.wait()


def per_device(sizes, strength, opacity, planck, old_populations, line_index, line_weight):
    bands, tiles, slabs = sizes
    depth, rows, cells = opacity.shape
    freqs = strength.shape[0]
    pairs = depth // 2
    chunks = bands * freqs // BATCH
    assert rows == 2 * ROWS and depth == ROWS and cells == bands * HALF and bands == 4
    f32 = jnp.float32
    hbm = pl.BlockSpec(memory_space=pltpu.HBM)
    vmem = pl.BlockSpec(memory_space=pltpu.VMEM)
    sem = pltpu.SemaphoreType.DMA
    tile = (ROWS, LANES)
    pops, source = pl.pallas_call(
        functools.partial(kernel, (bands, tiles, slabs, depth, freqs)),
        out_shape=(
            jax.ShapeDtypeStruct((LEVELS, depth, rows, cells // bands), f32),
            jax.ShapeDtypeStruct((freqs, depth, rows, cells), f32),
        ),
        in_specs=[hbm] * 6,
        out_specs=(vmem, vmem),
        scratch_shapes=[
            pltpu.SMEM((freqs,), f32),
            pltpu.SMEM((freqs,), jnp.int32),
            pltpu.SMEM((freqs,), f32),
            pltpu.VMEM((2 + LEVELS, depth, rows, LANES), f32),
            pltpu.VMEM((depth, rows, cells), f32),
            pltpu.VMEM((bands, 2) + tile, f32),
            pltpu.VMEM((bands, 1, LANES), jnp.int32),
            pltpu.SMEM((bands, 1, LANES), jnp.int32),
            pltpu.VMEM((2, 1 + LINES, pairs // 2) + tile, f32),
            pltpu.VMEM((2, 1 + LINES, pairs // 2) + tile, f32),
            pltpu.VMEM((depth, 3) + tile, f32),
            pltpu.VMEM((LINES, depth, 3) + tile, f32),
            pltpu.VMEM((depth, 2) + tile, f32),
            pltpu.VMEM((chunks, 2, BATCH) + tile, f32),
            pltpu.VMEM((2, chunks, BATCH) + tile, f32),
            pltpu.VMEM((chunks, 2, BATCH) + tile, f32),
            pltpu.VMEM((1 + bands * freqs, depth, 2) + tile, f32),
            pltpu.VMEM((bands, pairs, 4, 2) + tile, f32),
            pltpu.VMEM((LINES, depth, rows, cells), f32),
            sem((7,)),
            sem,
            sem((2, bands)),
            sem((2, bands)),
            sem((2,)),
            sem((2,)),
            sem((3, chunks)),
            sem((3, chunks)),
            sem((3, pairs)),
            sem((3, pairs)),
        ],
        compiler_params=pltpu.CompilerParams(
            collective_id=0, has_side_effects=True, vmem_limit_bytes=32 * 1024 * 1024
        ),
        cost_estimate=pl.CostEstimate(
            flops=60 * depth * rows * cells * freqs,
            bytes_accessed=16 * depth * rows * cells * 4,
            transcendentals=2 * depth * rows * cells * freqs,
        ),
    )(
        *(
            pltpu.with_memory_space_constraint(v, pltpu.HBM)
            for v in (strength, line_index, line_weight, opacity, planck, old_populations)
        )
    )
    return pl.pallas_call(
        write_out,
        out_shape=(
            jax.ShapeDtypeStruct(pops.shape, f32),
            jax.ShapeDtypeStruct(source.shape, f32),
        ),
        in_specs=[vmem] * 2,
        out_specs=(hbm, hbm),
        scratch_shapes=[sem((1 + freqs,))],
    )(
        pltpu.with_memory_space_constraint(pops, pltpu.VMEM),
        pltpu.with_memory_space_constraint(source, pltpu.VMEM),
    )


def solution(mesh):
    sizes = (mesh.shape["band"], mesh.shape["tile"], mesh.shape["slab"])
    in_specs = (
        P("band"),
        P("slab", "tile", None),
        P("slab", "tile", None),
        P(None, "slab", "tile", None),
        P("band"),
        P("band"),
    )
    out_specs = (P(None, "slab", "tile", "band"), P("band", "slab", "tile", None))
    return jax.shard_map(
        functools.partial(per_device, sizes),
        mesh=mesh,
        in_specs=in_specs,
        out_specs=out_specs,
        check_vma=False,
    )
```

```python
import functools

import jax
import jax.numpy as jnp
from jax import lax
from jax.experimental import pallas as pl
from jax.experimental.pallas import tpu as pltpu
from jax.sharding import PartitionSpec as P

MESH = pl.DeviceIdType.MESH
LINES = 5
LEVELS = 5
EPS_THERMAL = 0.1
COLLISION = 0.5
PATH_FACTOR = 1.25
TILT_SHARE = 0.4
LOWER_LEVEL = (0, 0, 1, 1, 2)
UPPER_LEVEL = (3, 4, 3, 4, 4)
LANES = 128
ROWS = 8
HALF = LANES // 2
BATCH = 8


def half_turn(v):
    return pltpu.roll(v, HALF, 1)


def kernel(
    sizes,
    strength_hbm,
    line_index_hbm,
    line_weight_hbm,
    opacity,
    planck,
    populations,
    pops_out,
    source_out,
    strength,
    line_index,
    line_weight,
    fields,
    planck_all,
    par_f,
    par_i,
    par_s,
    halo_out,
    halo_in,
    opac,
    src,
    plk,
    face_in,
    face_halo,
    face_out,
    acc,
    gathered,
    new_src,
    in_sem,
    idx_sem,
    par_send,
    par_recv,
    halo_send,
    halo_recv,
    face_send,
    face_recv,
    gat_send,
    gat_recv,
):
    bands, tiles, slabs, depth, freqs = sizes
    pairs = depth // 2
    subs = freqs // BATCH
    band = lax.axis_index("band")
    tile = lax.axis_index("tile")
    slab = lax.axis_index("slab")
    has_left = tile > 0
    has_right = tile < tiles - 1
    has_up = slab > 0
    has_down = slab < slabs - 1

    column = pl.multiple_of((band // 2) * LANES, LANES)
    loads = [
        pltpu.make_async_copy(opacity.at[:, :, pl.ds(column, LANES)], fields.at[0], in_sem.at[0]),
        pltpu.make_async_copy(planck.at[:, :, pl.ds(column, LANES)], fields.at[1], in_sem.at[1]),
        pltpu.make_async_copy(
            populations.at[:, :, :, pl.ds(column, LANES)], fields.at[pl.ds(2, LEVELS)], in_sem.at[2]
        ),
        pltpu.make_async_copy(strength_hbm, strength, in_sem.at[3]),
        pltpu.make_async_copy(line_index_hbm, line_index, in_sem.at[4]),
        pltpu.make_async_copy(line_weight_hbm, line_weight, in_sem.at[5]),
        pltpu.make_async_copy(planck, planck_all, in_sem.at[6]),
    ]
    for load in loads:
        load.start()

    barrier = pltpu.get_barrier_semaphore()
    for k in range(1, bands):
        pl.semaphore_signal(
            barrier, inc=1, device_id={"band": lax.rem(band + k, bands)}, device_id_type=MESH
        )
    expected = jnp.int32(bands - 1)
    for dt in (-1, 0, 1):
        for ds in (-1, 0, 1):
            if dt == 0 and ds == 0:
                continue
            there = (tile + dt >= 0) & (tile + dt < tiles) & (slab + ds >= 0) & (slab + ds < slabs)

            @pl.when(there)
            def _():
                pl.semaphore_signal(
                    barrier,
                    inc=1,
                    device_id={"tile": tile + dt, "slab": slab + ds},
                    device_id_type=MESH,
                )

            expected = expected + there.astype(jnp.int32)

    row = lax.broadcasted_iota(jnp.int32, (ROWS, LANES), 0)
    lane = lax.broadcasted_iota(jnp.int32, (ROWS, LANES), 1)
    left = lane < HALF
    own = (lane // HALF) == lax.rem(band, 2)
    top_left = left & (row == 0)
    low_right = jnp.logical_not(left) & (row == ROWS - 1)

    @pl.when(jnp.logical_not(has_left))
    def _():
        halo_in[0] = jnp.zeros(halo_in.shape[1:], jnp.float32)
        face_halo[0] = jnp.zeros(face_halo.shape[1:], jnp.float32)

    @pl.when(jnp.logical_not(has_right))
    def _():
        halo_in[1] = jnp.zeros(halo_in.shape[1:], jnp.float32)
        face_halo[1] = jnp.zeros(face_halo.shape[1:], jnp.float32)

    @pl.when(jnp.logical_not(has_up))
    def _():
        face_in[...] = jnp.zeros(face_in.shape, jnp.float32)
        face_halo[...] = jnp.zeros(face_halo.shape, jnp.float32)

    acc[0] = jnp.zeros(acc.shape[1:], jnp.float32)

    def par_copies(k):
        to = {"band": lax.rem(band + k, bands)}
        return (
            pltpu.make_async_remote_copy(
                src_ref=par_f.at[0],
                dst_ref=par_f.at[k],
                send_sem=par_send.at[0, k],
                recv_sem=par_recv.at[0, k],
                device_id=to,
                device_id_type=MESH,
            ),
            pltpu.make_async_remote_copy(
                src_ref=par_i.at[0],
                dst_ref=par_i.at[k],
                send_sem=par_send.at[1, k],
                recv_sem=par_recv.at[1, k],
                device_id=to,
                device_id_type=MESH,
            ),
        )

    for load in loads[:6]:
        load.wait()

    lane_row = lax.broadcasted_iota(jnp.int32, (1, LANES), 1)
    indices = jnp.zeros((1, LANES), jnp.int32)
    zero = jnp.zeros((ROWS, LANES), jnp.float32)
    rate, weight = zero, zero
    for f in range(freqs):
        here = row == f
        rate = jnp.where(here, -PATH_FACTOR * strength[f], rate)
        weight = jnp.where(here, line_weight[f] * (LINES / (2.0 * freqs * bands)), weight)
        indices = jnp.where(lane_row == f, line_index[f], indices)
    par_f[0, 0] = rate
    par_f[0, 1] = weight
    par_i[0] = indices

    def spread(v):
        return jnp.where(own, v, half_turn(v))

    def prepare(z, carry):
        for half in range(2):
            rows = pl.ds(half * ROWS, ROWS)
            p = spread(fields[1, z, rows])
            levels = [spread(fields[2 + i, z, rows]) for i in range(LEVELS)]
            opac[z, half] = spread(fields[0, z, rows])
            plk[z, half] = p
            for t in range(LINES):
                low, up = levels[LOWER_LEVEL[t]], levels[UPPER_LEVEL[t]]
                src[t, z, half] = EPS_THERMAL * p + (1.0 - EPS_THERMAL) * (up / (low + up))
        return carry

    for z in range(depth):
        prepare(z, 0)

    def layer(i, z, part):
        return opac[z, part] if i == 0 else src[i - 1, z, part]

    for i in range(1 + LINES):
        right, down = [], []
        for z in range(pairs):
            y = depth - 2 - z
            a, b = layer(i, z, 1), layer(i, z, 0)
            if y > z:
                a = jnp.where(row >= 1 + z, a, pltpu.roll(layer(i, y, 1), z + 1, 0))
                b = jnp.where(row <= y, b, pltpu.roll(layer(i, y, 0), y + 1, 0))
            right.append(a)
            down.append(b)
        for q in range(pairs // 2):
            halo_out[0, i, q] = jnp.where(left, right[q], right[q + pairs // 2])
            halo_out[1, i, q] = jnp.where(left, down[q + pairs // 2], down[q])

    pl.semaphore_wait(barrier, expected)
    for k in range(1, bands):
        for copy in par_copies(k):
            copy.start()

    def halo_copy(side):
        return pltpu.make_async_remote_copy(
            src_ref=halo_out.at[side],
            dst_ref=halo_in.at[side],
            send_sem=halo_send.at[side],
            recv_sem=halo_recv.at[side],
            device_id={"tile": tile + (1 if side == 0 else -1)},
            device_id_type=MESH,
        )

    @pl.when(has_right)
    def _():
        halo_copy(0).start()

    @pl.when(has_left)
    def _():
        halo_copy(1).start()

    for k in range(1, bands):
        for copy in par_copies(k):
            copy.wait_recv()
    to_scalars = pltpu.make_async_copy(par_i, par_s, idx_sem)
    to_scalars.start()

    @pl.when(has_left)
    def _():
        halo_copy(0).wait_recv()

    @pl.when(has_right)
    def _():
        halo_copy(1).wait_recv()

    for i in range(1 + LINES):
        for q in range(pairs // 2):
            a, b = halo_in[0, i, q], halo_in[1, i, q]
            shared = {q: jnp.where(left, a, b)}
            shared[q + pairs // 2] = half_turn(jnp.where(left, b, a))
            for z, tile_rows in shared.items():
                y = depth - 2 - z
                both = [(z, tile_rows)]
                if y > z:
                    moved = (pltpu.roll(tile_rows, y + 1, 0), pltpu.roll(tile_rows, z + 1, 0))
                    both.append((y, jnp.where(left, *moved)))
                for at, v in both:
                    if i == 0:
                        opac[at, 2] = v
                    else:
                        src[i - 1, at, 2] = v

    to_scalars.wait()

    def face_copies(chunk):
        def make(part, source, target, to):
            return pltpu.make_async_remote_copy(
                src_ref=source,
                dst_ref=target,
                send_sem=face_send.at[part, chunk],
                recv_sem=face_recv.at[part, chunk],
                device_id=to,
                device_id_type=MESH,
            )

        return (
            make(0, face_out.at[chunk], face_in.at[chunk], {"slab": slab + 1}),
            make(
                1,
                face_out.at[chunk, 1],
                face_halo.at[0, chunk],
                {"tile": tile + 1, "slab": slab + 1},
            ),
            make(
                2,
                face_out.at[chunk, 0],
                face_halo.at[1, chunk],
                {"tile": tile - 1, "slab": slab + 1},
            ),
        )

    def chunk_step(k, sub, latest):
        chunk = k * subs + sub
        main, to_right, to_left = face_copies(chunk)

        @pl.when(has_up)
        def _():
            main.wait_recv()

        @pl.when(has_up & has_left)
        def _():
            to_right.wait_recv()

        @pl.when(has_up & has_right)
        def _():
            to_left.wait_recv()

        states, rates, weights, indices, before, slots = [], [], [], [], [], []
        for f in range(BATCH):
            at = pl.ds(sub * BATCH + f, 1)
            rates.append(jnp.broadcast_to(par_f[k, 0, at], (ROWS, LANES)))
            weights.append(jnp.broadcast_to(par_f[k, 1, at], (ROWS, LANES)))
            line = par_s[k, 0, sub * BATCH + f]
            indices.append(line)
            slot = k * freqs + (sub * BATCH + f + 1)
            previous = latest[0]
            for t in range(1, LINES):
                previous = jnp.where(line == t, latest[t], previous)
            latest = [jnp.where(line == t, slot, latest[t]) for t in range(LINES)]
            before.append(previous)
            slots.append(slot)
            beyond = jnp.where(left, face_halo[0, chunk, f], face_halo[1, chunk, f])
            states.append((face_in[chunk, 0, f], face_in[chunk, 1, f], beyond))
        for z in range(depth):
            last = z == depth - 1
            o = [opac[z, i] for i in range(2 if last else 3)]
            for f in range(BATCH):
                one, two, out = states[f]
                d1, d2, dh = (pltpu.roll(v, 1, 0) for v in (one, two, out))
                u1, u2, uh = (pltpu.roll(v, ROWS - 1, 0) for v in (one, two, out))
                winds = [
                    jnp.where(top_left, dh, jnp.where(low_right, u2, jnp.where(left, d1, u1))),
                    jnp.where(top_left, d1, jnp.where(low_right, uh, jnp.where(left, d2, u2))),
                    jnp.where(left, dh, uh),
                ]
                fresh = []
                for i in range(len(o)):
                    s = src[indices[f], z, i]
                    a = jnp.exp(rates[f] * o[i])
                    mixed = (1.0 - TILT_SHARE) * states[f][i] + TILT_SHARE * winds[i]
                    fresh.append(s + a * (mixed - s))
                if last:
                    fresh.append(out)
                states[f] = tuple(fresh)
            for half in range(2):
                for f in range(BATCH):
                    acc[slots[f], z, half] = weights[f] * states[f][half]
        for f in range(BATCH):
            face_out[chunk, 0, f] = states[f][0]
            face_out[chunk, 1, f] = states[f][1]

        @pl.when(has_down & has_right)
        def _():
            to_right.start()

        @pl.when(has_down & has_left)
        def _():
            to_left.start()

        @pl.when(has_down)
        def _():
            main.start()

        for f in range(BATCH):
            acc[slots[f]] = acc[slots[f]] + acc[before[f]]
        return latest

    def group_step(k, latest):
        for sub in range(subs):
            latest = chunk_step(k, sub, latest)
        return tuple(latest)

    latest = lax.fori_loop(0, bands, group_step, (jnp.int32(0),) * LINES)

    beside = band + 1 - 2 * lax.rem(band, 2)
    across = lax.rem(band + 2, bands)
    corner = bands - 1 - band

    def gather_copy(kind, owner, zp, to):
        return pltpu.make_async_remote_copy(
            src_ref=gathered.at[owner, zp],
            dst_ref=gathered.at[owner, zp],
            send_sem=gat_send.at[kind, zp],
            recv_sem=gat_recv.at[kind, zp],
            device_id={"band": to},
            device_id_type=MESH,
        )

    def relax(zp, carry):
        for half in range(2):
            both = []
            for z in (zp, zp + pairs):
                p = COLLISION * plk[z, half]
                ratios = []
                for t in range(LINES):
                    j = acc[latest[t], z, half]
                    j = j + half_turn(j)
                    ratios.append((j + p) / ((1.0 + COLLISION) + j))
                one = 0.5 * (ratios[0] / ratios[2] + ratios[1] / ratios[3])
                levels = (one, ratios[1] / ratios[4], ratios[0], ratios[1])
                both.append(levels)
            for i in range(4):
                gathered[band, zp, i, half] = jnp.where(left, both[0][i], both[1][i])
        gather_copy(2, band, zp, corner).start()
        gather_copy(0, band, zp, beside).start()
        gather_copy(1, band, zp, across).start()
        return carry

    for zp in range(pairs):
        relax(zp, 0)

    loads[6].wait()

    def normalise(zp, carry):
        for half in range(2):
            rows = pl.ds(half * ROWS, ROWS)
            levels = [gathered[band, zp, i, half] for i in range(4)]
            scale = 1.0 / (1.0 + levels[0] + levels[1] + levels[2] + levels[3])
            for i, v in enumerate([scale] + [scale * level for level in levels]):
                pops_out[i, zp, rows] = v[:, :HALF]
                pops_out[i, zp + pairs, rows] = half_turn(v)[:, :HALF]
        return carry

    lax.fori_loop(0, pairs, normalise, 0)

    def finish_two(q, carry):
        gather_copy(0, beside, 2 * q, beside).wait_recv()
        gather_copy(1, across, 2 * q, across).wait_recv()
        gather_copy(2, corner, 2 * q, corner).wait_recv()
        finish(2 * q)
        gather_copy(0, beside, 2 * q + 1, beside).wait_recv()
        gather_copy(1, across, 2 * q + 1, across).wait_recv()
        gather_copy(2, corner, 2 * q + 1, corner).wait_recv()
        finish(2 * q + 1)
        return carry

    def finish(zp):
        for pair in range(bands // 2):
            columns = slice(pair * LANES, (pair + 1) * LANES)
            for half in range(2):
                rows = pl.ds(half * ROWS, ROWS)
                lines = []
                for b in (2 * pair, 2 * pair + 1):
                    levels = [1.0] + [gathered[b, zp, i, half] for i in range(4)]
                    lines.append(
                        [
                            levels[UPPER_LEVEL[t]] / (levels[LOWER_LEVEL[t]] + levels[UPPER_LEVEL[t]])
                            for t in range(LINES)
                        ]
                    )
                first = EPS_THERMAL * planck_all[zp, rows, columns]
                second = EPS_THERMAL * planck_all[zp + pairs, rows, columns]
                for t in range(LINES):
                    even, odd = lines[0][t], lines[1][t]
                    new_src[t, zp, rows, columns] = first + (1.0 - EPS_THERMAL) * jnp.where(
                        left, even, half_turn(odd)
                    )
                    new_src[t, zp + pairs, rows, columns] = second + (
                        1.0 - EPS_THERMAL
                    ) * jnp.where(left, half_turn(even), odd)
        for f in range(freqs):
            t = line_index[f]
            source_out[f, zp] = new_src[t, zp]
            source_out[f, zp + pairs] = new_src[t, zp + pairs]

    lax.fori_loop(0, pairs // 2, finish_two, 0)

    for k in range(1, bands):
        for copy in par_copies(k):
            copy.wait_send()

    @pl.when(has_right)
    def _():
        halo_copy(0).wait_send()

    @pl.when(has_left)
    def _():
        halo_copy(1).wait_send()

    def drain(chunk, carry):
        main, to_right, to_left = face_copies(chunk)

        @pl.when(has_down)
        def _():
            main.wait_send()

        @pl.when(has_down & has_right)
        def _():
            to_right.wait_send()

        @pl.when(has_down & has_left)
        def _():
            to_left.wait_send()

        return carry

    lax.fori_loop(0, bands * subs, drain, 0)

    def drain_gather(zp, carry):
        gather_copy(0, band, zp, beside).wait_send()
        gather_copy(1, band, zp, across).wait_send()
        gather_copy(2, band, zp, corner).wait_send()
        return carry

    lax.fori_loop(0, pairs, drain_gather, 0)


def write_out(pops, source, pops_hbm, source_hbm, sem):
    copies = [pltpu.make_async_copy(pops, pops_hbm, sem.at[0])]
    for f in range(source.shape[0]):
        copies.append(pltpu.make_async_copy(source.at[f], source_hbm.at[f], sem.at[1 + f]))
    for copy in copies:
        copy.start()
    for copy in copies:
        copy.wait()


def per_device(sizes, strength, opacity, planck, old_populations, line_index, line_weight):
    bands, tiles, slabs = sizes
    depth, rows, cells = opacity.shape
    freqs = strength.shape[0]
    pairs = depth // 2
    chunks = bands * freqs // BATCH
    assert rows == 2 * ROWS and depth == ROWS and cells == bands * HALF and bands == 4
    f32 = jnp.float32
    hbm = pl.BlockSpec(memory_space=pltpu.HBM)
    vmem = pl.BlockSpec(memory_space=pltpu.VMEM)
    sem = pltpu.SemaphoreType.DMA
    tile = (ROWS, LANES)
    pops, source = pl.pallas_call(
        functools.partial(kernel, (bands, tiles, slabs, depth, freqs)),
        out_shape=(
            jax.ShapeDtypeStruct((LEVELS, depth, rows, cells // bands), f32),
            jax.ShapeDtypeStruct((freqs, depth, rows, cells), f32),
        ),
        in_specs=[hbm] * 6,
        out_specs=(vmem, vmem),
        scratch_shapes=[
            pltpu.SMEM((freqs,), f32),
            pltpu.SMEM((freqs,), jnp.int32),
            pltpu.SMEM((freqs,), f32),
            pltpu.VMEM((2 + LEVELS, depth, rows, LANES), f32),
            pltpu.VMEM((depth, rows, cells), f32),
            pltpu.VMEM((bands, 2) + tile, f32),
            pltpu.VMEM((bands, 1, LANES), jnp.int32),
            pltpu.SMEM((bands, 1, LANES), jnp.int32),
            pltpu.VMEM((2, 1 + LINES, pairs // 2) + tile, f32),
            pltpu.VMEM((2, 1 + LINES, pairs // 2) + tile, f32),
            pltpu.VMEM((depth, 3) + tile, f32),
            pltpu.VMEM((LINES, depth, 3) + tile, f32),
            pltpu.VMEM((depth, 2) + tile, f32),
            pltpu.VMEM((chunks, 2, BATCH) + tile, f32),
            pltpu.VMEM((2, chunks, BATCH) + tile, f32),
            pltpu.VMEM((chunks, 2, BATCH) + tile, f32),
            pltpu.VMEM((1 + bands * freqs, depth, 2) + tile, f32),
            pltpu.VMEM((bands, pairs, 4, 2) + tile, f32),
            pltpu.VMEM((LINES, depth, rows, cells), f32),
            sem((7,)),
            sem,
            sem((2, bands)),
            sem((2, bands)),
            sem((2,)),
            sem((2,)),
            sem((3, chunks)),
            sem((3, chunks)),
            sem((3, pairs)),
            sem((3, pairs)),
        ],
        compiler_params=pltpu.CompilerParams(
            collective_id=0, has_side_effects=True, vmem_limit_bytes=32 * 1024 * 1024
        ),
        cost_estimate=pl.CostEstimate(
            flops=60 * depth * rows * cells * freqs,
            bytes_accessed=16 * depth * rows * cells * 4,
            transcendentals=2 * depth * rows * cells * freqs,
        ),
    )(
        *(
            pltpu.with_memory_space_constraint(v, pltpu.HBM)
            for v in (strength, line_index, line_weight, opacity, planck, old_populations)
        )
    )
    return pl.pallas_call(
        write_out,
        out_shape=(
            jax.ShapeDtypeStruct(pops.shape, f32),
            jax.ShapeDtypeStruct(source.shape, f32),
        ),
        in_specs=[vmem] * 2,
        out_specs=(hbm, hbm),
        scratch_shapes=[sem((1 + freqs,))],
    )(
        pltpu.with_memory_space_constraint(pops, pltpu.VMEM),
        pltpu.with_memory_space_constraint(source, pltpu.VMEM),
    )


def solution(mesh):
    sizes = (mesh.shape["band"], mesh.shape["tile"], mesh.shape["slab"])
    in_specs = (
        P("band"),
        P("slab", "tile", None),
        P("slab", "tile", None),
        P(None, "slab", "tile", None),
        P("band"),
        P("band"),
    )
    out_specs = (P(None, "slab", "tile", "band"), P("band", "slab", "tile", None))
    return jax.shard_map(
        functools.partial(per_device, sizes),
        mesh=mesh,
        in_specs=in_specs,
        out_specs=out_specs,
        check_vma=False,
    )
```
